32 devices in a mesh: groups: 2 (over x), dp: 2 (over core), tensor: 8 (over z, y).
Axes of the slice: x: 2, y: 2, z: 4, core: 2. Of those that a mesh axis runs over, the one named last changes fastest.
Arguments:
- suffix_acts: bfloat16 [4, 768, 4096], P(('groups', 'dp'), 'tensor'), parts along dimension 0, may hold values from -6 to 6
- suffix_lens: int32 [4, 16], P(('groups', 'dp')), parts along dimension 0, may hold values from 8 to 48, as said below
- hit_holder: int32 [4, 16], P('groups'), parts along dimension 0, may hold values from 0 to 1
- hit_slot: int32 [4, 16], P('groups'), parts along dimension 0, may hold values from 0 to 15
- cache_states: float32 [64, 128, 64, 128], P(('groups', 'dp'), 'tensor'), parts along dimension 0, may hold values from -0.8 to 0.8
- cache_conv_x: bfloat16 [64, 3, 8192], P(('groups', 'dp'), None, 'tensor'), parts along dimension 0, may hold values from -6 to 6
- cache_conv_bc: bfloat16 [64, 3, 1024], P(('groups', 'dp'), None, 'tensor'), parts along dimension 0, may hold values from -6 to 6
- w_in_x: bfloat16 [4096, 8192], P(None, 'tensor'), may hold values from -0.09375 to 0.09375
- w_in_z: bfloat16 [4096, 8192], P(None, 'tensor'), may hold values from -0.09375 to 0.09375
- w_in_bc: bfloat16 [4096, 1024], P(None, 'tensor'), may hold values from -0.09375 to 0.09375
- w_in_dt: bfloat16 [4096, 128], P(None, 'tensor'), may hold values from -0.09375 to 0.09375
- conv_x: float32 [4, 8192], P(None, 'tensor'), may hold values from -3 to 3
- conv_bc: float32 [4, 1024], P(None, 'tensor'), may hold values from -3 to 3
- dt_bias: float32 [128], P('tensor'), may hold values from -2 to 0.5
- decay_rate: float32 [128], P('tensor'), may hold values from 0.004 to 0.15
- skip_gain: float32 [128], P('tensor'), may hold values from 0.5 to 1.5
- norm_gain: float32 [8192], P('tensor'), may hold values from 0.5 to 1.5
- w_out: bfloat16 [8192, 4096], P('tensor'), may hold values from -0.0625 to 0.0625
Outputs:
- mixed_out: bfloat16 [4, 768, 4096], P(('groups', 'dp'), 'tensor'), parts along dimension 0
- new_states: float32 [4, 16, 128, 64, 128], P(('groups', 'dp'), None, 'tensor'), parts along dimension 0
- new_tail_x: bfloat16 [4, 16, 3, 8192], P(('groups', 'dp'), None, None, 'tensor'), parts along dimension 0
- new_tail_bc: bfloat16 [4, 16, 3, 1024], P(('groups', 'dp'), None, None, 'tensor'), parts along dimension 0
The draws below stay inside these ranges and needn't reach their ends.
There are 2 independent parts, one for each index of `groups`. The reference program is written for one: setup_inputs(seed, part) draws one part's arguments, and reference() takes and returns one part's arrays. A program takes and returns all parts, laid end to end along the dimension named above; an argument that names none is the same for every part. Nothing has to cross between parts.
Inputs may be any that keep to these rules, and one draw needn't show every extreme that they name: `suffix_lens`: every replica has a request of exactly 48 suffix tokens and one of 8.
All inputs are finite; a program needn't handle non-finite values.
Results may differ from the reference program's by a relative error of at most 0.0077.
Values may be sent and summed in bfloat16 or wider, within the bound.
A program may use at most 192 MiB of HBM per device.

```python
import math
import jax
import jax.numpy as jnp
from jax import lax

D = 4096
HEADS = 128
HDIM = 64
NSTATE = 128
GROUPS = 4
KCONV = 4
SUF = 48
REQ = 16
SLOTS = 16
DI = 8192
KT = 3
BC = 1024
N_DP = 2


def draw_suffix_lens(key, part):
    key = jax.random.fold_in(key, 11)
    key = jax.random.fold_in(key, part)
    first_key, second_key = jax.random.split(key)
    lengths = jax.random.randint(first_key, (N_DP, REQ), 8, SUF + 1, dtype=jnp.int32)
    picked = jax.random.randint(second_key, (N_DP,), 0, REQ, dtype=jnp.int32)
    replicas = jnp.arange(N_DP, dtype=jnp.int32)
    lengths = lengths.at[replicas, picked].set(SUF)
    lengths = lengths.at[replicas, (picked + 1) % REQ].set(8)
    return lengths


def with_ends(values, rng, smallest, largest):
    longest = values.shape.index(max(values.shape))
    spots = []
    for shift in (0, 1):
        where = [jax.random.randint(jax.random.fold_in(rng, axis), (), 0, length) for axis, length in enumerate(values.shape)]
        where[longest] = (where[longest] + shift) % values.shape[longest]
        spots.append(tuple(where))
    return values.at[spots[0]].set(smallest).at[spots[1]].set(largest)


def levels(key, shape, pieces, least, top_value):
    factor_of, own = 1.0, jax.random.fold_in(key, 6)
    for dim, shards_of in pieces:
        draws = jnp.exp(jax.random.uniform(jax.random.fold_in(own, dim), (shards_of,), jnp.float32, least / len(pieces), top_value / len(pieces)))
        factor_of = factor_of * jnp.repeat(draws, shape[dim] // shards_of).reshape([-1 if axis == dim else 1 for axis in range(len(shape))])
    return factor_of


def noise(own_key, shape, deviation, reach, shards=(), kind=jnp.bfloat16):
    result = deviation * jax.random.normal(own_key, shape, jnp.float32)
    if shards:
        result = result * levels(own_key, shape, shards, -0.22, 0.18)
    return jnp.clip(result, -reach, reach).astype(kind)


def setup_inputs(seed: int = 0, part: int = 0) -> dict:
    key_of = jax.random.split(jax.random.key(seed), 19)
    own_keys = jax.random.split(jax.random.fold_in(key_of[18], part), 19)
    suffix_acts = noise(own_keys[0], (N_DP, REQ * SUF, D), 1.0, 6.0, ((0, 2), (1, 8)))
    suffix_lens = draw_suffix_lens(jax.random.fold_in(jax.random.fold_in(key_of[18], part), 71), part)
    hit_holder = with_ends(jax.random.randint(own_keys[2], (N_DP, REQ), 0, N_DP), jax.random.fold_in(own_keys[2], 1), 0, N_DP - 1).astype(jnp.int32)
    hit_slot = with_ends(jax.random.randint(own_keys[3], (N_DP, REQ), 0, SLOTS), jax.random.fold_in(own_keys[3], 1), 0, SLOTS - 1).astype(jnp.int32)
    cache_states = noise(own_keys[4], (N_DP * SLOTS, HEADS, HDIM, NSTATE), 0.1, 0.8, ((0, 2), (1, 8)), jnp.float32)
    cache_conv_x = noise(own_keys[5], (N_DP * SLOTS, KT, DI), 1.0, 6.0, ((0, 2), (2, 8)))
    cache_conv_bc = noise(own_keys[6], (N_DP * SLOTS, KT, BC), 1.0, 6.0, ((0, 2), (2, 8)))
    w_in_x = noise(key_of[7], (D, DI), D ** -0.5, 0.09375, ((1, 8),))
    w_in_z = noise(key_of[8], (D, DI), D ** -0.5, 0.09375, ((1, 8),))
    w_in_bc = noise(key_of[9], (D, BC), D ** -0.5, 0.09375, ((1, 8),))
    w_in_dt = noise(key_of[10], (D, HEADS), D ** -0.5, 0.09375, ((1, 8),))
    conv_x = noise(key_of[11], (KCONV, DI), KCONV ** -0.5, 3.0, ((1, 8),), jnp.float32)
    conv_bc = noise(key_of[12], (KCONV, BC), KCONV ** -0.5, 3.0, ((1, 8),), jnp.float32)
    dt_bias = jnp.clip(-2.0 + 2.5 * jax.random.uniform(key_of[13], (HEADS,), jnp.float32) ** levels(key_of[13], (HEADS,), ((0, 8),), -0.2, 0.2), -2.0, 0.5)
    decay_rate = jnp.clip(jnp.exp(math.log(0.15) - 3.624341 * jax.random.uniform(key_of[14], (HEADS,), jnp.float32) ** levels(key_of[14], (HEADS,), ((0, 8),), -0.2, 0.2)), 0.004, 0.15)
    skip_gain = jnp.clip(0.5 + 1.0 * jax.random.uniform(key_of[15], (HEADS,), jnp.float32) ** levels(key_of[15], (HEADS,), ((0, 8),), -0.2, 0.2), 0.5, 1.5)
    norm_gain = jnp.clip(1.0 + 0.1 * jax.random.normal(key_of[16], (DI,), jnp.float32), 0.5, 1.5)
    w_out = noise(key_of[17], (DI, D), DI ** -0.5, 0.0625, ((0, 8),))
    return dict(suffix_acts=suffix_acts, suffix_lens=suffix_lens, hit_holder=hit_holder, hit_slot=hit_slot, cache_states=cache_states, cache_conv_x=cache_conv_x, cache_conv_bc=cache_conv_bc, w_in_x=w_in_x, w_in_z=w_in_z, w_in_bc=w_in_bc, w_in_dt=w_in_dt, conv_x=conv_x, conv_bc=conv_bc, dt_bias=dt_bias, decay_rate=decay_rate, skip_gain=skip_gain, norm_gain=norm_gain, w_out=w_out)


highest = lax.Precision.HIGHEST
epsilon = 1e-05

def causal_conv(tail_rows, raw_rows, weight):
    extended = jnp.concatenate([tail_rows, raw_rows], axis=-2)
    seq_len = raw_rows.shape[-2]
    running = jnp.zeros(raw_rows.shape, jnp.float32)
    for offset in range(weight.shape[0]):
        running = running + weight[offset] * extended[..., offset:offset + seq_len, :].astype(jnp.float32)
    return (extended, lax.optimization_barrier(jax.nn.silu(running).astype(jnp.bfloat16)))

def last_rows(extended, lengths):
    index_rows = lengths[..., None] + jnp.arange(KT, dtype=jnp.int32)
    return jnp.take_along_axis(extended, index_rows[..., None], axis=-2)

def scan_block(values, scores, b_rows, c_rows, step_size, decay_rate, start_state, skip_gain):
    log_step = -decay_rate * step_size
    log_sum = jnp.cumsum(log_step, axis=-2)
    position = jnp.arange(values.shape[-3], dtype=jnp.int32)
    causal = position[:, None] >= position[None, :]
    log_gap = log_sum[..., :, None, :] - log_sum[..., None, :, :]
    decay_mat = jnp.where(causal[:, :, None], jnp.exp(jnp.minimum(log_gap, 0.0)), 0.0)
    weights = scores * decay_mat * step_size[..., None, :, :]
    outputs = jnp.einsum('...tsh,...shp->...thp', weights, values, precision=highest)
    carried = jnp.einsum('...thn,...hpn->...thp', c_rows, start_state, precision=highest)
    outputs = outputs + jnp.exp(log_sum)[..., None] * carried + skip_gain[:, None] * values
    weight_tail = jnp.exp(log_sum[..., -1:, :] - log_sum) * step_size
    scaled_vals = weight_tail[..., None] * values
    end_state = jnp.exp(log_sum[..., -1, :])[..., None, None] * start_state
    end_state = end_state + jnp.einsum('...shp,...shn->...hpn', scaled_vals, b_rows, precision=highest)
    return (outputs, end_state)

def reference(suffix_acts, suffix_lens, hit_holder, hit_slot, cache_states, cache_conv_x, cache_conv_bc, w_in_x, w_in_z, w_in_bc, w_in_dt, conv_x, conv_bc, dt_bias, decay_rate, skip_gain, norm_gain, w_out):
    wanted = (hit_holder * SLOTS + hit_slot).astype(jnp.int32)
    start_state = cache_states[wanted]
    tail_x = cache_conv_x[wanted]
    tail_bc = cache_conv_bc[wanted]
    flat_rows = suffix_acts.reshape(N_DP * REQ * SUF, D)
    raw_x = jnp.dot(flat_rows, w_in_x, preferred_element_type=jnp.float32).astype(jnp.bfloat16)
    raw_z = jnp.dot(flat_rows, w_in_z, preferred_element_type=jnp.float32).astype(jnp.bfloat16)
    raw_bc = jnp.dot(flat_rows, w_in_bc, preferred_element_type=jnp.float32).astype(jnp.bfloat16)
    raw_x, raw_z, raw_bc = lax.optimization_barrier((raw_x, raw_z, raw_bc))
    raw_dt = jnp.dot(flat_rows, w_in_dt, preferred_element_type=jnp.float32)
    raw_x = raw_x.reshape(N_DP, REQ, SUF, DI)
    raw_z = raw_z.reshape(N_DP, REQ, SUF, DI)
    raw_bc = raw_bc.reshape(N_DP, REQ, SUF, BC)
    raw_dt = raw_dt.reshape(N_DP, REQ, SUF, HEADS)
    ext_x, act_x = causal_conv(tail_x, raw_x, conv_x)
    ext_bc, act_bc = causal_conv(tail_bc, raw_bc, conv_bc)
    new_tail_x = last_rows(ext_x, suffix_lens)
    new_tail_bc = last_rows(ext_bc, suffix_lens)
    half_width = GROUPS * NSTATE
    b_all = act_bc[..., :half_width].reshape(N_DP, REQ, SUF, GROUPS, NSTATE).astype(jnp.float32)
    c_all = act_bc[..., half_width:].reshape(N_DP, REQ, SUF, GROUPS, NSTATE).astype(jnp.float32)
    group_scores = jnp.einsum('...tgn,...sgn->...tsg', c_all, b_all, precision=highest)
    head_group = jnp.arange(HEADS, dtype=jnp.int32) % GROUPS
    scores = group_scores[..., head_group]
    b_heads = b_all[:, :, :, head_group]
    c_heads = c_all[:, :, :, head_group]
    live = jnp.arange(SUF, dtype=jnp.int32)[None, None, :] < suffix_lens[:, :, None]
    step_size = jnp.where(live[..., None], jax.nn.softplus(raw_dt + dt_bias), 0.0)
    values = act_x.astype(jnp.float32).reshape(N_DP, REQ, SUF, HEADS, HDIM)
    outputs, new_states = scan_block(values, scores, b_heads, c_heads, step_size, decay_rate, start_state, skip_gain)
    gated = outputs * jax.nn.silu(raw_z.astype(jnp.float32)).reshape(N_DP, REQ, SUF, HEADS, HDIM)
    grouped = gated.reshape(N_DP, REQ, SUF, HEADS // GROUPS, GROUPS, HDIM)
    mean_square = lax.optimization_barrier(jnp.mean(grouped * grouped, axis=(-3, -1)))
    scaled = (grouped * lax.rsqrt(mean_square + epsilon)[..., None, :, None]).reshape(N_DP, REQ, SUF, DI) * norm_gain
    normed = jnp.where(live[..., None], scaled, 0.0).astype(jnp.bfloat16).reshape(N_DP * REQ * SUF, DI)
    mixed_out = jnp.dot(normed, w_out, preferred_element_type=jnp.float32).astype(jnp.bfloat16)
    return (mixed_out.reshape(N_DP, REQ * SUF, D), new_states, new_tail_x, new_tail_bc)
```

```python
import jax
import jax.numpy as jnp
from jax import lax
from jax.experimental import pallas as pl
from jax.experimental.pallas import tpu as pltpu
from jax.sharding import PartitionSpec as P

HEADS = 128
HDIM = 64
NSTATE = 128
GROUPS = 4
KT = 3


highest = lax.Precision.HIGHEST
epsilon = 1e-05


def causal_conv(tail_rows, raw_rows, weight):
    extended = jnp.concatenate([tail_rows, raw_rows], axis=-2)
    seq_len = raw_rows.shape[-2]
    running = jnp.zeros(raw_rows.shape, jnp.float32)
    for offset in range(weight.shape[0]):
        running = running + weight[offset] * extended[..., offset : offset + seq_len, :].astype(
            jnp.float32
        )
    return (extended, lax.optimization_barrier(jax.nn.silu(running).astype(jnp.bfloat16)))


def last_rows(extended, lengths):
    index_rows = lengths[..., None] + jnp.arange(KT, dtype=jnp.int32)
    return jnp.take_along_axis(extended, index_rows[..., None], axis=-2)


def scan_block(values, scores, b_rows, c_rows, step_size, decay_rate, start_state, skip_gain):
    log_step = -decay_rate * step_size
    log_sum = jnp.cumsum(log_step, axis=-2)
    position = jnp.arange(values.shape[-3], dtype=jnp.int32)
    causal = position[:, None] >= position[None, :]
    log_gap = log_sum[..., :, None, :] - log_sum[..., None, :, :]
    decay_mat = jnp.where(causal[:, :, None], jnp.exp(jnp.minimum(log_gap, 0.0)), 0.0)
    weights = scores * decay_mat * step_size[..., None, :, :]
    outputs = jnp.einsum("...tsh,...shp->...thp", weights, values, precision=highest)
    carried = jnp.einsum("...thn,...hpn->...thp", c_rows, start_state, precision=highest)
    outputs = outputs + jnp.exp(log_sum)[..., None] * carried + skip_gain[:, None] * values
    weight_tail = jnp.exp(log_sum[..., -1:, :] - log_sum) * step_size
    scaled_vals = weight_tail[..., None] * values
    end_state = jnp.exp(log_sum[..., -1, :])[..., None, None] * start_state
    end_state = end_state + jnp.einsum(
        "...shp,...shn->...hpn", scaled_vals, b_rows, precision=highest
    )
    return (outputs, end_state)


def local_plain(
    suffix_acts,
    suffix_lens,
    hit_holder,
    hit_slot,
    cache_states,
    cache_conv_x,
    cache_conv_bc,
    w_in_x,
    w_in_z,
    w_in_bc,
    w_in_dt,
    conv_x,
    conv_bc,
    dt_bias,
    decay_rate,
    skip_gain,
    norm_gain,
    w_out,
):
    replica = lax.axis_index("dp")
    lengths = suffix_lens[0]
    requests = lengths.shape[0]
    from_me = hit_holder == replica
    keep_mask = from_me[:, :, None, None]
    send_state = jnp.where(from_me[:, :, None, None, None], cache_states[hit_slot], 0.0)
    send_x = jnp.where(keep_mask, cache_conv_x[hit_slot].astype(jnp.float32), 0.0)
    send_bc = jnp.where(keep_mask, cache_conv_bc[hit_slot].astype(jnp.float32), 0.0)
    got_state, got_x, got_bc = (
        lax.all_to_all(send_state, "dp", split_axis=0, concat_axis=0, tiled=True),
        lax.all_to_all(send_x, "dp", split_axis=0, concat_axis=0, tiled=True),
        lax.all_to_all(send_bc, "dp", split_axis=0, concat_axis=0, tiled=True),
    )
    start_state = jnp.sum(got_state, axis=0)
    tail_x = jnp.sum(got_x, axis=0).astype(jnp.bfloat16)
    tail_bc = jnp.sum(got_bc, axis=0).astype(jnp.bfloat16)
    local_x = w_in_x.shape[1]
    local_bc = w_in_bc.shape[1]
    local_heads = w_in_dt.shape[1]
    flat_rows = lax.all_gather(suffix_acts, "tensor", axis=1, tiled=True)[0]
    pieces = [
        jnp.dot(flat_rows, w_in_x, preferred_element_type=jnp.float32),
        jnp.dot(flat_rows, w_in_z, preferred_element_type=jnp.float32),
        jnp.dot(flat_rows, w_in_bc, preferred_element_type=jnp.float32),
        jnp.dot(flat_rows, w_in_dt, preferred_element_type=jnp.float32),
    ]
    projected = jnp.concatenate(pieces, axis=-1)[None]
    projected = projected[0].reshape(requests, -1, projected.shape[-1])
    seq_len = projected.shape[1]
    raw_x = projected[..., :local_x].astype(jnp.bfloat16)
    raw_z = projected[..., local_x : 2 * local_x].astype(jnp.bfloat16)
    raw_bc = projected[..., 2 * local_x : 2 * local_x + local_bc].astype(jnp.bfloat16)
    raw_x, raw_z, raw_bc = lax.optimization_barrier((raw_x, raw_z, raw_bc))
    raw_dt = projected[..., 2 * local_x + local_bc :]
    ext_x, act_x = causal_conv(tail_x, raw_x, conv_x)
    ext_bc, act_bc = causal_conv(tail_bc, raw_bc, conv_bc)
    new_tail_x = last_rows(ext_x, lengths)
    new_tail_bc = last_rows(ext_bc, lengths)
    every_bc = lax.all_gather(act_bc, "tensor", axis=2, tiled=True)
    half_width = GROUPS * NSTATE
    b_all = every_bc[..., :half_width].reshape(requests, seq_len, GROUPS, NSTATE)
    c_all = every_bc[..., half_width:].reshape(requests, seq_len, GROUPS, NSTATE)
    head_ids = lax.axis_index("tensor") * local_heads + jnp.arange(local_heads, dtype=jnp.int32)
    head_group = head_ids % GROUPS
    group_scores = jnp.einsum("qtgn,qsgn->qtsg", c_all, b_all, preferred_element_type=jnp.float32)
    scores = jnp.take(group_scores, head_group, axis=3)
    b_heads = jnp.take(b_all, head_group, axis=2).astype(jnp.float32)
    c_heads = jnp.take(c_all, head_group, axis=2).astype(jnp.float32)
    live = jnp.arange(seq_len, dtype=jnp.int32)[None, :] < lengths[:, None]
    step_size = jnp.where(live[..., None], jax.nn.softplus(raw_dt + dt_bias), 0.0)
    values = act_x.astype(jnp.float32).reshape(requests, seq_len, local_heads, HDIM)
    outputs, new_states = scan_block(
        values, scores, b_heads, c_heads, step_size, decay_rate, start_state, skip_gain
    )
    gated = outputs * jax.nn.silu(raw_z.astype(jnp.float32)).reshape(
        requests, seq_len, local_heads, HDIM
    )
    per_head = jnp.sum(gated * gated, axis=-1)
    member = (head_group[:, None] == jnp.arange(GROUPS, dtype=jnp.int32)[None, :]).astype(
        jnp.float32
    )
    group_part = jnp.sum(per_head[..., :, None] * member, axis=-2)
    group_total = lax.psum(group_part, "tensor")
    mean_square = jnp.sum(group_total[..., None, :] * member, axis=-1) / (HEADS // GROUPS * HDIM)
    scaled = (
        gated * lax.rsqrt(mean_square + epsilon)[..., None] * norm_gain.reshape(local_heads, HDIM)
    )
    normed = (
        jnp.where(live[..., None, None], scaled, 0.0)
        .astype(jnp.bfloat16)
        .reshape(requests * seq_len, local_x)
    )
    mixed_out = lax.psum_scatter(
        jnp.dot(normed, w_out, preferred_element_type=jnp.float32),
        "tensor",
        scatter_dimension=0,
        tiled=True,
    )
    return (
        mixed_out.astype(jnp.bfloat16)[None],
        new_states[None],
        new_tail_x[None],
        new_tail_bc[None],
    )


def scan_kernel(
    slot_ref,
    mine_ref,
    len_ref,
    raw_x_ref,
    raw_z_ref,
    dt_ref,
    dt_t_ref,
    bc_ref,
    own_x_ref,
    got_x_ref,
    own_state_ref,
    got_state_ref,
    conv_ref,
    bias_ref,
    bias_t_ref,
    decay_ref,
    decay_t_ref,
    skip_ref,
    gated_ref,
    part_ref,
    state_ref,
    tail_ref,
    ext_ref,
):
    q = pl.program_id(0)
    mine = mine_ref[q] == 1
    length = len_ref[q]
    seq, width = raw_x_ref.shape
    heads = dt_ref.shape[-1]
    pad = 8
    tail = jnp.where(
        mine, own_x_ref[0].astype(jnp.float32), got_x_ref[0].astype(jnp.float32)
    )
    ext_ref[0:pad, :] = jnp.zeros((pad, width), jnp.float32)
    ext_ref[pl.ds(pad - KT, KT), :] = tail
    ext_ref[pl.ds(pad, seq), :] = raw_x_ref[...].astype(jnp.float32)
    picked = lax.broadcasted_iota(jnp.int32, (pad, pad + seq), 1) == (
        lax.broadcasted_iota(jnp.int32, (pad, pad + seq), 0) + (pad - KT + length)
    )
    tail_ref[0] = jnp.dot(
        picked.astype(jnp.bfloat16),
        ext_ref[0 : pad + seq, :].astype(jnp.bfloat16),
        preferred_element_type=jnp.float32,
    )[:KT].astype(jnp.bfloat16)

    step = jnp.where(
        lax.broadcasted_iota(jnp.int32, (seq, heads), 0) < length,
        jax.nn.softplus(dt_ref[0] + bias_ref[...]),
        0.0,
    )
    step_t = jnp.where(
        lax.broadcasted_iota(jnp.int32, (heads, seq), 1) < length,
        jax.nn.softplus(dt_t_ref[0] + bias_t_ref[...]),
        0.0,
    )
    rows = lax.broadcasted_iota(jnp.int32, (seq, seq), 0)
    cols = lax.broadcasted_iota(jnp.int32, (seq, seq), 1)
    causal = rows >= cols
    log_sum = jnp.dot(
        causal.astype(jnp.float32),
        -decay_ref[...] * step,
        precision=highest,
        preferred_element_type=jnp.float32,
    )
    log_sum_t = jnp.dot(
        -decay_t_ref[...] * step_t,
        (rows <= cols).astype(jnp.float32),
        precision=highest,
        preferred_element_type=jnp.float32,
    )
    half = GROUPS * NSTATE
    contract_last = (((1,), (1,)), ((), ()))
    contract_first = (((0,), (0,)), ((), ()))
    b_rows = [bc_ref[:, g * NSTATE : (g + 1) * NSTATE] for g in range(GROUPS)]
    c_rows = [bc_ref[:, half + g * NSTATE : half + (g + 1) * NSTATE] for g in range(GROUPS)]
    scores = [
        lax.dot_general(
            c_rows[g], b_rows[g], contract_last, preferred_element_type=jnp.float32
        )
        for g in range(GROUPS)
    ]
    c_pair = [jnp.concatenate([c_rows[g], c_rows[g + 1]], axis=0) for g in range(0, GROUPS, 2)]
    b_pair = [jnp.concatenate([b_rows[g], b_rows[g + 1]], axis=1) for g in range(0, GROUPS, 2)]
    lanes = 2 * HDIM
    first = lax.broadcasted_iota(jnp.int32, (seq, lanes), 1) < HDIM
    squares = [jnp.zeros((seq, lanes), jnp.float32) for _ in range(GROUPS // 2)]
    for pair in range(heads // 2):
        h = 2 * pair
        g = h % GROUPS
        span = slice(pair * lanes, (pair + 1) * lanes)
        running = conv_ref[0:1, span] * ext_ref[pad - KT : pad - KT + seq, span]
        for k in range(1, KT + 1):
            running = running + (
                conv_ref[k : k + 1, span] * ext_ref[pad - KT + k : pad - KT + k + seq, span]
            )
        act = (running / (1.0 + jnp.exp(-running))).astype(jnp.bfloat16)
        values = act.astype(jnp.float32)
        wide = [jnp.broadcast_to(log_sum[:, h + i : h + i + 1], (seq, lanes)) for i in range(2)]
        mats = []
        for i in range(2):
            gap = jnp.minimum(wide[i][:, :seq] - log_sum_t[h + i : h + i + 1, :], 0.0)
            decay = jnp.where(causal, jnp.exp(gap), 0.0)
            mats.append(
                (scores[g + i] * decay * step_t[h + i : h + i + 1, :]).astype(jnp.bfloat16)
            )
        inner = jnp.dot(
            jnp.concatenate(mats, axis=0), act, preferred_element_type=jnp.float32
        )
        start = jnp.where(
            mine,
            own_state_ref[0, h : h + 2],
            got_state_ref[0, h : h + 2].astype(jnp.float32),
        ).reshape(lanes, NSTATE)
        carried = lax.dot_general(
            c_pair[g // 2],
            start.astype(jnp.bfloat16),
            contract_last,
            preferred_element_type=jnp.float32,
        )
        log_pair = jnp.where(first, wide[0], wide[1])
        step_pair = jnp.where(first, step[:, h : h + 1], step[:, h + 1 : h + 2])
        out = jnp.where(first, inner[:seq], inner[seq:]) + jnp.exp(log_pair) * jnp.where(
            first, carried[:seq], carried[seq:]
        )
        out = out + skip_ref[:, span] * values
        z = raw_z_ref[:, span].astype(jnp.float32)
        gated = out * (z / (1.0 + jnp.exp(-z)))
        gated_ref[:, span] = gated
        squares[g // 2] = squares[g // 2] + gated * gated
        last = log_pair[seq - 1 : seq, :]
        scaled = (jnp.exp(last - log_pair) * step_pair * values).astype(jnp.bfloat16)
        added = lax.dot_general(
            scaled, b_pair[g // 2], contract_first, preferred_element_type=jnp.float32
        )
        for i in range(2):
            fade = jnp.exp(wide[i][seq - 1 : seq, :])
            state_ref[0, h + i] = (
                fade * start[i * HDIM : (i + 1) * HDIM]
                + added[i * HDIM : (i + 1) * HDIM, i * NSTATE : (i + 1) * NSTATE]
            )
    total = []
    for value in squares:
        total.append(jnp.sum(jnp.where(first, value, 0.0), axis=1, keepdims=True))
        total.append(jnp.sum(jnp.where(first, 0.0, value), axis=1, keepdims=True))
    part_ref[...] = jnp.concatenate(total, axis=1)


def scan_call(
    slot, mine, lengths, raw_x, raw_z, dt, dt_t, every_bc, own_x, got_x, own_state, got_state,
    conv_x, dt_bias, decay_rate, skip_gain,
):
    requests = lengths.shape[0]
    heads = dt.shape[-1]
    seq = dt.shape[1]
    width = raw_x.shape[1]
    whole = lambda *shape: pl.BlockSpec(shape, lambda q, *_: (0,) * len(shape))
    row = lambda n: pl.BlockSpec((seq, n), lambda q, *_: (q, 0))
    by_q = lambda *shape: pl.BlockSpec((1, *shape), lambda q, *_: (q,) + (0,) * len(shape))
    by_slot = lambda *shape: pl.BlockSpec(
        (1, *shape), lambda q, slots, *_: (slots[q],) + (0,) * len(shape)
    )
    return pl.pallas_call(
        scan_kernel,
        grid_spec=pltpu.PrefetchScalarGridSpec(
            num_scalar_prefetch=3,
            grid=(requests,),
            in_specs=[
                row(width),
                row(width),
                by_q(seq, heads),
                by_q(heads, seq),
                row(every_bc.shape[1]),
                by_slot(KT, width),
                by_q(KT, width),
                by_slot(heads, HDIM, NSTATE),
                by_q(heads, HDIM, NSTATE),
                whole(*conv_x.shape),
                whole(1, heads),
                whole(heads, 1),
                whole(1, heads),
                whole(heads, 1),
                whole(1, width),
            ],
            out_specs=[
                row(width),
                row(GROUPS),
                by_q(heads, HDIM, NSTATE),
                by_q(KT, width),
            ],
            scratch_shapes=[pltpu.VMEM((seq + 16, width), jnp.float32)],
        ),
        out_shape=[
            jax.ShapeDtypeStruct((requests * seq, width), jnp.float32),
            jax.ShapeDtypeStruct((requests * seq, GROUPS), jnp.float32),
            jax.ShapeDtypeStruct((requests, heads, HDIM, NSTATE), jnp.float32),
            jax.ShapeDtypeStruct((requests, KT, width), jnp.bfloat16),
        ],
        compiler_params=pltpu.CompilerParams(vmem_limit_bytes=32 * 1024 * 1024),
        cost_estimate=pl.CostEstimate(
            flops=2 * requests * heads * seq * (seq * HDIM + 2 * HDIM * NSTATE),
            bytes_accessed=requests * heads * HDIM * NSTATE * 10,
            transcendentals=requests * seq * width * 4,
        ),
        name="scan",
    )(
        slot, mine, lengths, raw_x, raw_z, dt, dt_t, every_bc, own_x, got_x, own_state, got_state,
        conv_x, dt_bias[None], dt_bias[:, None], decay_rate[None], decay_rate[:, None],
        jnp.repeat(skip_gain, HDIM)[None],
    )


def local(
    suffix_acts,
    suffix_lens,
    hit_holder,
    hit_slot,
    cache_states,
    cache_conv_x,
    cache_conv_bc,
    w_in_x,
    w_in_z,
    w_in_bc,
    w_in_dt,
    conv_x,
    conv_bc,
    dt_bias,
    decay_rate,
    skip_gain,
    norm_gain,
    w_out,
):
    replica = lax.axis_index("dp")
    lengths = suffix_lens[0]
    requests = lengths.shape[0]
    slot = jnp.where(replica == 0, hit_slot[0], hit_slot[1])
    other_slot = jnp.where(replica == 0, hit_slot[1], hit_slot[0])
    mine = jnp.where(replica == 0, hit_holder[0], hit_holder[1]) == replica
    swap = [(0, 1), (1, 0)]
    got_bc = lax.ppermute(cache_conv_bc[other_slot], "dp", swap)
    got_x = lax.ppermute(cache_conv_x[other_slot], "dp", swap)
    got_state = lax.ppermute(cache_states[other_slot].astype(jnp.bfloat16), "dp", swap)
    tail_bc = jnp.where(mine[:, None, None], cache_conv_bc[slot], got_bc)
    local_x = w_in_x.shape[1]
    local_bc = w_in_bc.shape[1]
    local_heads = w_in_dt.shape[1]
    flat_rows = lax.all_gather(suffix_acts, "tensor", axis=1, tiled=True)[0]
    seq_len = flat_rows.shape[0] // requests
    raw_bc = jnp.dot(flat_rows, w_in_bc, preferred_element_type=jnp.float32)
    raw_bc = raw_bc.astype(jnp.bfloat16).reshape(requests, seq_len, local_bc)
    ext_bc, act_bc = causal_conv(tail_bc, raw_bc, conv_bc)
    every_bc = lax.all_gather(
        act_bc.reshape(requests * seq_len, local_bc), "tensor", axis=1, tiled=True
    )
    raw_x = jnp.dot(flat_rows, w_in_x, preferred_element_type=jnp.float32).astype(jnp.bfloat16)
    raw_z = jnp.dot(flat_rows, w_in_z, preferred_element_type=jnp.float32).astype(jnp.bfloat16)
    raw_dt = jnp.dot(flat_rows, w_in_dt, preferred_element_type=jnp.float32)
    dt = raw_dt.reshape(requests, seq_len, local_heads)
    new_tail_bc = last_rows(ext_bc, lengths)
    gated, part, new_states, new_tail_x = scan_call(
        slot, mine.astype(jnp.int32), lengths, raw_x, raw_z, dt, dt.transpose(0, 2, 1), every_bc,
        cache_conv_x, got_x, cache_states, got_state, conv_x, dt_bias, decay_rate, skip_gain,
    )
    total = lax.psum(part, "tensor")
    inverse = lax.rsqrt(total / (HEADS // GROUPS * HDIM) + epsilon)
    live = jnp.arange(seq_len, dtype=jnp.int32)[None, :] < lengths[:, None]
    inverse = jnp.where(live.reshape(-1)[:, None], inverse, 0.0)
    inverse = jnp.repeat(jnp.tile(inverse, (1, local_heads // GROUPS)), HDIM, axis=1)
    normed = (gated * inverse * norm_gain).astype(jnp.bfloat16)
    mixed_out = lax.psum_scatter(
        jnp.dot(normed, w_out, preferred_element_type=jnp.float32).astype(jnp.bfloat16),
        "tensor",
        scatter_dimension=0,
        tiled=True,
    )
    return (
        mixed_out[None],
        new_states[None],
        new_tail_x[None],
        new_tail_bc[None],
    )


def solution(mesh):
    regular = mesh.shape["tensor"] == 8
    return jax.shard_map(
        local if regular else local_plain,
        mesh=mesh,
        in_specs=(
            P(("groups", "dp"), "tensor", None),
            P(("groups", "dp"), None),
            P("groups", None),
            P("groups", None),
            P(("groups", "dp"), "tensor", None, None),
            P(("groups", "dp"), None, "tensor"),
            P(("groups", "dp"), None, "tensor"),
            P(None, "tensor"),
            P(None, "tensor"),
            P(None, "tensor"),
            P(None, "tensor"),
            P(None, "tensor"),
            P(None, "tensor"),
            P("tensor"),
            P("tensor"),
            P("tensor"),
            P("tensor"),
            P("tensor", None),
        ),
        out_specs=(
            P(("groups", "dp"), "tensor", None),
            P(("groups", "dp"), None, "tensor", None, None),
            P(("groups", "dp"), None, None, "tensor"),
            P(("groups", "dp"), None, None, "tensor"),
        ),
        check_vma=False,
    )
```

```python
import jax
import jax.numpy as jnp
from jax import lax
from jax.experimental import pallas as pl
from jax.experimental.pallas import tpu as pltpu
from jax.sharding import PartitionSpec as P

HEADS = 128
HDIM = 64
NSTATE = 128
GROUPS = 4
KT = 3


highest = lax.Precision.HIGHEST
epsilon = 1e-05


def causal_conv(tail_rows, raw_rows, weight):
    extended = jnp.concatenate([tail_rows, raw_rows], axis=-2)
    seq_len = raw_rows.shape[-2]
    running = jnp.zeros(raw_rows.shape, jnp.float32)
    for offset in range(weight.shape[0]):
        running = running + weight[offset] * extended[..., offset : offset + seq_len, :].astype(
            jnp.float32
        )
    return (extended, lax.optimization_barrier(jax.nn.silu(running).astype(jnp.bfloat16)))


def last_rows(extended, lengths):
    index_rows = lengths[..., None] + jnp.arange(KT, dtype=jnp.int32)
    return jnp.take_along_axis(extended, index_rows[..., None], axis=-2)


def scan_block(values, scores, b_rows, c_rows, step_size, decay_rate, start_state, skip_gain):
    log_step = -decay_rate * step_size
    log_sum = jnp.cumsum(log_step, axis=-2)
    position = jnp.arange(values.shape[-3], dtype=jnp.int32)
    causal = position[:, None] >= position[None, :]
    log_gap = log_sum[..., :, None, :] - log_sum[..., None, :, :]
    decay_mat = jnp.where(causal[:, :, None], jnp.exp(jnp.minimum(log_gap, 0.0)), 0.0)
    weights = scores * decay_mat * step_size[..., None, :, :]
    outputs = jnp.einsum("...tsh,...shp->...thp", weights, values, precision=highest)
    carried = jnp.einsum("...thn,...hpn->...thp", c_rows, start_state, precision=highest)
    outputs = outputs + jnp.exp(log_sum)[..., None] * carried + skip_gain[:, None] * values
    weight_tail = jnp.exp(log_sum[..., -1:, :] - log_sum) * step_size
    scaled_vals = weight_tail[..., None] * values
    end_state = jnp.exp(log_sum[..., -1, :])[..., None, None] * start_state
    end_state = end_state + jnp.einsum(
        "...shp,...shn->...hpn", scaled_vals, b_rows, precision=highest
    )
    return (outputs, end_state)


def local_plain(
    suffix_acts,
    suffix_lens,
    hit_holder,
    hit_slot,
    cache_states,
    cache_conv_x,
    cache_conv_bc,
    w_in_x,
    w_in_z,
    w_in_bc,
    w_in_dt,
    conv_x,
    conv_bc,
    dt_bias,
    decay_rate,
    skip_gain,
    norm_gain,
    w_out,
):
    replica = lax.axis_index("dp")
    lengths = suffix_lens[0]
    requests = lengths.shape[0]
    from_me = hit_holder == replica
    keep_mask = from_me[:, :, None, None]
    send_state = jnp.where(from_me[:, :, None, None, None], cache_states[hit_slot], 0.0)
    send_x = jnp.where(keep_mask, cache_conv_x[hit_slot].astype(jnp.float32), 0.0)
    send_bc = jnp.where(keep_mask, cache_conv_bc[hit_slot].astype(jnp.float32), 0.0)
    got_state, got_x, got_bc = (
        lax.all_to_all(send_state, "dp", split_axis=0, concat_axis=0, tiled=True),
        lax.all_to_all(send_x, "dp", split_axis=0, concat_axis=0, tiled=True),
        lax.all_to_all(send_bc, "dp", split_axis=0, concat_axis=0, tiled=True),
    )
    start_state = jnp.sum(got_state, axis=0)
    tail_x = jnp.sum(got_x, axis=0).astype(jnp.bfloat16)
    tail_bc = jnp.sum(got_bc, axis=0).astype(jnp.bfloat16)
    local_x = w_in_x.shape[1]
    local_bc = w_in_bc.shape[1]
    local_heads = w_in_dt.shape[1]
    flat_rows = lax.all_gather(suffix_acts, "tensor", axis=1, tiled=True)[0]
    pieces = [
        jnp.dot(flat_rows, w_in_x, preferred_element_type=jnp.float32),
        jnp.dot(flat_rows, w_in_z, preferred_element_type=jnp.float32),
        jnp.dot(flat_rows, w_in_bc, preferred_element_type=jnp.float32),
        jnp.dot(flat_rows, w_in_dt, preferred_element_type=jnp.float32),
    ]
    projected = jnp.concatenate(pieces, axis=-1)[None]
    projected = projected[0].reshape(requests, -1, projected.shape[-1])
    seq_len = projected.shape[1]
    raw_x = projected[..., :local_x].astype(jnp.bfloat16)
    raw_z = projected[..., local_x : 2 * local_x].astype(jnp.bfloat16)
    raw_bc = projected[..., 2 * local_x : 2 * local_x + local_bc].astype(jnp.bfloat16)
    raw_x, raw_z, raw_bc = lax.optimization_barrier((raw_x, raw_z, raw_bc))
    raw_dt = projected[..., 2 * local_x + local_bc :]
    ext_x, act_x = causal_conv(tail_x, raw_x, conv_x)
    ext_bc, act_bc = causal_conv(tail_bc, raw_bc, conv_bc)
    new_tail_x = last_rows(ext_x, lengths)
    new_tail_bc = last_rows(ext_bc, lengths)
    every_bc = lax.all_gather(act_bc, "tensor", axis=2, tiled=True)
    half_width = GROUPS * NSTATE
    b_all = every_bc[..., :half_width].reshape(requests, seq_len, GROUPS, NSTATE)
    c_all = every_bc[..., half_width:].reshape(requests, seq_len, GROUPS, NSTATE)
    head_ids = lax.axis_index("tensor") * local_heads + jnp.arange(local_heads, dtype=jnp.int32)
    head_group = head_ids % GROUPS
    group_scores = jnp.einsum("qtgn,qsgn->qtsg", c_all, b_all, preferred_element_type=jnp.float32)
    scores = jnp.take(group_scores, head_group, axis=3)
    b_heads = jnp.take(b_all, head_group, axis=2).astype(jnp.float32)
    c_heads = jnp.take(c_all, head_group, axis=2).astype(jnp.float32)
    live = jnp.arange(seq_len, dtype=jnp.int32)[None, :] < lengths[:, None]
    step_size = jnp.where(live[..., None], jax.nn.softplus(raw_dt + dt_bias), 0.0)
    values = act_x.astype(jnp.float32).reshape(requests, seq_len, local_heads, HDIM)
    outputs, new_states = scan_block(
        values, scores, b_heads, c_heads, step_size, decay_rate, start_state, skip_gain
    )
    gated = outputs * jax.nn.silu(raw_z.astype(jnp.float32)).reshape(
        requests, seq_len, local_heads, HDIM
    )
    per_head = jnp.sum(gated * gated, axis=-1)
    member = (head_group[:, None] == jnp.arange(GROUPS, dtype=jnp.int32)[None, :]).astype(
        jnp.float32
    )
    group_part = jnp.sum(per_head[..., :, None] * member, axis=-2)
    group_total = lax.psum(group_part, "tensor")
    mean_square = jnp.sum(group_total[..., None, :] * member, axis=-1) / (HEADS // GROUPS * HDIM)
    scaled = (
        gated * lax.rsqrt(mean_square + epsilon)[..., None] * norm_gain.reshape(local_heads, HDIM)
    )
    normed = (
        jnp.where(live[..., None, None], scaled, 0.0)
        .astype(jnp.bfloat16)
        .reshape(requests * seq_len, local_x)
    )
    mixed_out = lax.psum_scatter(
        jnp.dot(normed, w_out, preferred_element_type=jnp.float32),
        "tensor",
        scatter_dimension=0,
        tiled=True,
    )
    return (
        mixed_out.astype(jnp.bfloat16)[None],
        new_states[None],
        new_tail_x[None],
        new_tail_bc[None],
    )


LINE = 4


def place():
    me = lax.axis_index("tensor")
    return me, me // 2, me % 2


def nearest(z, k):
    low = z < 2
    near = jnp.where(low, z, LINE - 1 - z)
    pick = jnp.where(near == 0, k, (1, 0, 2, 3)[k])
    return jnp.where(low, pick, LINE - 1 - pick)


def signal(device):
    pl.semaphore_signal(
        pltpu.get_barrier_semaphore(),
        inc=1,
        device_id={"tensor": device},
        device_id_type=pl.DeviceIdType.MESH,
    )


def remote(source, target, send_sem, recv_sem, device):
    return pltpu.make_async_remote_copy(
        src_ref=source,
        dst_ref=target,
        send_sem=send_sem,
        recv_sem=recv_sem,
        device_id={"tensor": device},
        device_id_type=pl.DeviceIdType.MESH,
    )


def project_kernel(
    acts_ref, w_x_ref, w_bc_ref, w_dt_ref, rows_ref, x_ref, bc_ref, dt_ref,
    held, x_buf, bc_buf, dt_buf, load_sem, store_sem, line_send, line_recv, side_send, side_recv,
):
    me, z, y = place()
    part = acts_ref.shape[0]
    side = me + 1 - 2 * y
    loads = [
        pltpu.make_async_copy(acts_ref, held.at[pl.ds(me * part, part)], load_sem.at[0]),
        pltpu.make_async_copy(w_x_ref, x_buf, load_sem.at[1]),
        pltpu.make_async_copy(w_bc_ref, bc_buf, load_sem.at[2]),
        pltpu.make_async_copy(w_dt_ref, dt_buf, load_sem.at[3]),
    ]
    for load in loads:
        load.start()
    signal(side)

    @pl.when(z < LINE - 1)
    def _():
        signal(me + 2)

    @pl.when(z > 0)
    def _():
        signal(me - 2)

    ends = (z == 0) | (z == LINE - 1)
    pl.semaphore_wait(pltpu.get_barrier_semaphore(), jnp.where(ends, 2, 3))

    def spot(plane, column):
        return held.at[pl.ds((2 * plane + column) * part, part)]

    def up(plane):
        return remote(
            spot(plane, y), spot(plane, y), line_send.at[0, plane], line_recv.at[plane], me + 2
        )

    def down(plane):
        return remote(
            spot(plane, y), spot(plane, y), line_send.at[1, plane], line_recv.at[plane], me - 2
        )

    def across(plane):
        return remote(
            spot(plane, y), spot(plane, y), side_send.at[plane], side_recv.at[plane], side
        )

    def arrived(plane, column, sem):
        return remote(spot(plane, column), spot(plane, column), line_send.at[0, 0], sem, side)

    loads[0].wait()
    for k in range(LINE + 1):
        if k < LINE:
            plane = nearest(z, k)
            if k > 0:
                arrived(plane, y, line_recv.at[plane]).wait_recv()

            @pl.when((plane <= z) & (z < LINE - 1))
            def _():
                up(plane).start()

            @pl.when((plane >= z) & (z > 0))
            def _():
                down(plane).start()

            across(plane).start()
        if k == 1:
            for load in loads[1:]:
                load.wait()
        if k > 0:
            plane = nearest(z, k - 1)
            arrived(plane, 1 - y, side_recv.at[plane]).wait_recv()
            span = pl.ds(plane * (2 * part), 2 * part)
            pltpu.make_async_copy(held.at[span], rows_ref.at[span], store_sem.at[k - 1]).start()
            bc_ref[span, :] = jnp.dot(
                held[span, :], bc_buf[...], preferred_element_type=jnp.float32
            ).astype(jnp.bfloat16)
            dt_ref[span, :] = jnp.dot(
                held[span, :], dt_buf[...], preferred_element_type=jnp.float32
            )
            tile = 256

            def step(j, carry):
                columns = pl.ds(pl.multiple_of(j * tile, tile), tile)
                x_ref[span, columns] = jnp.dot(
                    held[span, :], x_buf[:, columns], preferred_element_type=jnp.float32
                ).astype(jnp.bfloat16)
                return carry

            lax.fori_loop(0, x_ref.shape[1] // tile, step, 0)
    for k in range(LINE):
        plane = nearest(z, k)

        @pl.when((plane <= z) & (z < LINE - 1))
        def _():
            up(plane).wait_send()

        @pl.when((plane >= z) & (z > 0))
        def _():
            down(plane).wait_send()

        across(plane).wait_send()
        span = pl.ds(plane * (2 * part), 2 * part)
        pltpu.make_async_copy(held.at[span], rows_ref.at[span], store_sem.at[k]).wait()


def project_call(acts, w_x, w_bc, w_dt):
    part, depth = acts.shape
    rows = part * 2 * LINE
    vmem = pl.BlockSpec(memory_space=pltpu.VMEM)
    hbm = pl.BlockSpec(memory_space=pl.ANY)
    dma = pltpu.SemaphoreType.DMA
    return pl.pallas_call(
        project_kernel,
        in_specs=[hbm] * 4,
        out_specs=[hbm, vmem, vmem, vmem],
        out_shape=[
            jax.ShapeDtypeStruct((rows, depth), jnp.bfloat16),
            jax.ShapeDtypeStruct((rows, w_x.shape[1]), jnp.bfloat16),
            jax.ShapeDtypeStruct((rows, w_bc.shape[1]), jnp.bfloat16),
            jax.ShapeDtypeStruct((rows, w_dt.shape[1]), jnp.float32),
        ],
        scratch_shapes=[
            pltpu.VMEM((rows, depth), jnp.bfloat16),
            pltpu.VMEM(w_x.shape, jnp.bfloat16),
            pltpu.VMEM(w_bc.shape, jnp.bfloat16),
            pltpu.VMEM(w_dt.shape, jnp.bfloat16),
            dma((4,)),
            dma((LINE,)),
            dma((2, LINE)),
            dma((LINE,)),
            dma((LINE,)),
            dma((LINE,)),
        ],
        compiler_params=pltpu.CompilerParams(
            collective_id=0, has_side_effects=True, vmem_limit_bytes=40 * 1024 * 1024
        ),
        cost_estimate=pl.CostEstimate(
            flops=2 * rows * depth * w_x.shape[1],
            bytes_accessed=4 * rows * depth + 2 * depth * w_x.shape[1],
            transcendentals=0,
        ),
        name="gather_project",
    )(acts, w_x, w_bc, w_dt)


def output_kernel(
    gated_ref, part_ref, live_ref, member_ref, gain_ref, w_ref, out_ref,
    parts, normed, w_buf, own, side_out, side_in, line_out, line_in,
    load_sem, part_send, part_recv, side_send, side_recv, line_send, line_recv,
):
    me, z, y = place()
    peers = 2 * LINE
    rows, width = gated_ref.shape
    chunk = rows // peers
    side = me + 1 - 2 * y
    load = pltpu.make_async_copy(w_ref, w_buf, load_sem)
    load.start()
    for hop in range(1, peers):
        signal(lax.rem(me + hop, peers))
    pl.semaphore_wait(pltpu.get_barrier_semaphore(), peers - 1)
    sends = []
    for hop in range(1, peers):
        send = remote(
            part_ref, parts.at[hop], part_send.at[hop], part_recv.at[hop], lax.rem(me + hop, peers)
        )
        send.start()
        sends.append(send)
    total = part_ref[...]
    for hop in range(1, peers):
        sends[hop - 1].wait_recv()
        total = total + parts[hop]
    inverse = lax.rsqrt(total / (HEADS // GROUPS * HDIM) + epsilon)
    inverse = jnp.where(live_ref[...] > 0.0, inverse, 0.0)
    high = inverse.astype(jnp.bfloat16)
    low = (inverse - high.astype(jnp.float32)).astype(jnp.bfloat16)
    both = jnp.concatenate([high, low], axis=0)
    block = rows // 2
    for i in range(2):
        scale = lax.dot_general(
            both[:, i * block : (i + 1) * block],
            member_ref[...],
            (((0,), (0,)), ((), ())),
            preferred_element_type=jnp.float32,
        )
        span = slice(i * block, (i + 1) * block)
        normed[span, :] = (gated_ref[span, :] * scale * gain_ref[...]).astype(jnp.bfloat16)
    load.wait()

    def across(plane):
        return remote(
            side_out.at[plane], side_in.at[plane], side_send.at[plane], side_recv.at[plane], side
        )

    def along(plane):
        toward = jnp.where(plane > z, me + 2, me - 2)
        slot = jnp.where((plane < z) & (plane == z - 1), LINE, plane)
        return remote(
            line_out.at[plane], line_in.at[slot], line_send.at[plane], line_recv.at[slot], toward
        )

    def line_arrived(slot):
        return remote(line_in.at[slot], line_in.at[slot], line_send.at[0], line_recv.at[slot], side)

    tile = 512
    tiles = w_buf.shape[1] // tile
    for k in range(LINE - 1, -1, -1):
        plane = nearest(z, k)
        span = pl.ds(plane * (2 * chunk), 2 * chunk)

        def step(j, carry):
            columns = pl.ds(pl.multiple_of(j * tile, tile), tile)
            result = jnp.dot(
                normed[span, :], w_buf[:, columns], preferred_element_type=jnp.float32
            )
            own[plane, :, columns] = jnp.where(y == 0, result[:chunk], result[chunk:])
            side_out[plane, :, columns] = jnp.where(
                y == 0, result[chunk:], result[:chunk]
            ).astype(jnp.bfloat16)
            return carry

        lax.fori_loop(0, tiles, step, 0)
        across(plane).start()
    for k in range(LINE - 1, 0, -1):
        plane = nearest(z, k)
        across(plane).wait_recv()
        joined = ((plane > z) & (z > 0)) | ((plane < z) & (z < LINE - 1))

        @pl.when(joined)
        def _():
            line_arrived(plane).wait_recv()
            line_out[plane] = (
                own[plane]
                + side_in[plane].astype(jnp.float32)
                + line_in[plane].astype(jnp.float32)
            ).astype(jnp.bfloat16)

        @pl.when(jnp.logical_not(joined))
        def _():
            line_out[plane] = (own[plane] + side_in[plane].astype(jnp.float32)).astype(
                jnp.bfloat16
            )

        along(plane).start()
    across(z).wait_recv()
    own[z] = own[z] + side_in[z].astype(jnp.float32)

    @pl.when(z > 0)
    def _():
        line_arrived(z).wait_recv()
        own[z] = own[z] + line_in[z].astype(jnp.float32)

    @pl.when(z < LINE - 1)
    def _():
        line_arrived(LINE).wait_recv()
        own[z] = own[z] + line_in[LINE].astype(jnp.float32)

    out_ref[...] = own[z].astype(jnp.bfloat16)
    for send in sends:
        send.wait_send()
    for k in range(LINE):
        plane = nearest(z, k)
        across(plane).wait_send()
        if k > 0:
            along(plane).wait_send()


def output_call(gated, part, live, member, gain, w_out):
    rows, width = gated.shape
    depth = w_out.shape[1]
    peers = 2 * LINE
    chunk = rows // peers
    vmem = pl.BlockSpec(memory_space=pltpu.VMEM)
    dma = pltpu.SemaphoreType.DMA
    return pl.pallas_call(
        output_kernel,
        in_specs=[vmem] * 5 + [pl.BlockSpec(memory_space=pl.ANY)],
        out_specs=vmem,
        out_shape=jax.ShapeDtypeStruct((chunk, depth), jnp.bfloat16),
        scratch_shapes=[
            pltpu.VMEM((peers, *part.shape), jnp.float32),
            pltpu.VMEM((rows, width), jnp.bfloat16),
            pltpu.VMEM(w_out.shape, jnp.bfloat16),
            pltpu.VMEM((LINE, chunk, depth), jnp.float32),
            pltpu.VMEM((LINE, chunk, depth), jnp.bfloat16),
            pltpu.VMEM((LINE, chunk, depth), jnp.bfloat16),
            pltpu.VMEM((LINE, chunk, depth), jnp.bfloat16),
            pltpu.VMEM((LINE + 1, chunk, depth), jnp.bfloat16),
            dma,
            dma((peers,)),
            dma((peers,)),
            dma((LINE,)),
            dma((LINE,)),
            dma((LINE,)),
            dma((LINE + 1,)),
        ],
        compiler_params=pltpu.CompilerParams(
            collective_id=1, has_side_effects=True, vmem_limit_bytes=52 * 1024 * 1024
        ),
        cost_estimate=pl.CostEstimate(
            flops=2 * rows * width * depth,
            bytes_accessed=2 * width * depth + 4 * rows * width,
            transcendentals=0,
        ),
        name="norm_project_reduce",
    )(gated, part, live, member, gain, w_out)


def scan_kernel(
    slot_ref,
    mine_ref,
    len_ref,
    raw_x_ref,
    raw_z_ref,
    dt_ref,
    dt_t_ref,
    bc_ref,
    own_x_ref,
    got_x_ref,
    own_state_ref,
    got_state_ref,
    conv_ref,
    bias_ref,
    bias_t_ref,
    decay_ref,
    decay_t_ref,
    skip_ref,
    gated_ref,
    part_ref,
    state_ref,
    tail_ref,
    ext_ref,
):
    q = pl.program_id(0)
    mine = mine_ref[q] == 1
    length = len_ref[q]
    seq, width = raw_x_ref.shape
    heads = dt_ref.shape[-1]
    pad = 8
    tail = jnp.where(
        mine, own_x_ref[0].astype(jnp.float32), got_x_ref[0].astype(jnp.float32)
    )
    ext_ref[0:pad, :] = jnp.zeros((pad, width), jnp.float32)
    ext_ref[pl.ds(pad - KT, KT), :] = tail
    ext_ref[pl.ds(pad, seq), :] = raw_x_ref[...].astype(jnp.float32)
    picked = lax.broadcasted_iota(jnp.int32, (pad, pad + seq), 1) == (
        lax.broadcasted_iota(jnp.int32, (pad, pad + seq), 0) + (pad - KT + length)
    )
    tail_ref[0] = jnp.dot(
        picked.astype(jnp.bfloat16),
        ext_ref[0 : pad + seq, :].astype(jnp.bfloat16),
        preferred_element_type=jnp.float32,
    )[:KT].astype(jnp.bfloat16)

    step = jnp.where(
        lax.broadcasted_iota(jnp.int32, (seq, heads), 0) < length,
        jax.nn.softplus(dt_ref[0] + bias_ref[...]),
        0.0,
    )
    step_t = jnp.where(
        lax.broadcasted_iota(jnp.int32, (heads, seq), 1) < length,
        jax.nn.softplus(dt_t_ref[0] + bias_t_ref[...]),
        0.0,
    )
    rows = lax.broadcasted_iota(jnp.int32, (seq, seq), 0)
    cols = lax.broadcasted_iota(jnp.int32, (seq, seq), 1)
    causal = rows >= cols
    log_sum = jnp.dot(
        causal.astype(jnp.float32),
        -decay_ref[...] * step,
        precision=highest,
        preferred_element_type=jnp.float32,
    )
    log_sum_t = jnp.dot(
        -decay_t_ref[...] * step_t,
        (rows <= cols).astype(jnp.float32),
        precision=highest,
        preferred_element_type=jnp.float32,
    )
    half = GROUPS * NSTATE
    contract_last = (((1,), (1,)), ((), ()))
    contract_first = (((0,), (0,)), ((), ()))
    b_rows = [bc_ref[:, g * NSTATE : (g + 1) * NSTATE] for g in range(GROUPS)]
    c_rows = [bc_ref[:, half + g * NSTATE : half + (g + 1) * NSTATE] for g in range(GROUPS)]
    scores = [
        lax.dot_general(
            c_rows[g], b_rows[g], contract_last, preferred_element_type=jnp.float32
        )
        for g in range(GROUPS)
    ]
    c_pair = [jnp.concatenate([c_rows[g], c_rows[g + 1]], axis=0) for g in range(0, GROUPS, 2)]
    b_pair = [jnp.concatenate([b_rows[g], b_rows[g + 1]], axis=1) for g in range(0, GROUPS, 2)]
    lanes = 2 * HDIM
    first = lax.broadcasted_iota(jnp.int32, (seq, lanes), 1) < HDIM
    squares = [jnp.zeros((seq, lanes), jnp.float32) for _ in range(GROUPS // 2)]
    for pair in range(heads // 2):
        h = 2 * pair
        g = h % GROUPS
        span = slice(pair * lanes, (pair + 1) * lanes)
        running = conv_ref[0:1, span] * ext_ref[pad - KT : pad - KT + seq, span]
        for k in range(1, KT + 1):
            running = running + (
                conv_ref[k : k + 1, span] * ext_ref[pad - KT + k : pad - KT + k + seq, span]
            )
        act = (running / (1.0 + jnp.exp(-running))).astype(jnp.bfloat16)
        values = act.astype(jnp.float32)
        wide = [jnp.broadcast_to(log_sum[:, h + i : h + i + 1], (seq, lanes)) for i in range(2)]
        mats = []
        for i in range(2):
            gap = jnp.minimum(wide[i][:, :seq] - log_sum_t[h + i : h + i + 1, :], 0.0)
            decay = jnp.where(causal, jnp.exp(gap), 0.0)
            mats.append(
                (scores[g + i] * decay * step_t[h + i : h + i + 1, :]).astype(jnp.bfloat16)
            )
        inner = jnp.dot(
            jnp.concatenate(mats, axis=0), act, preferred_element_type=jnp.float32
        )
        start = jnp.where(
            mine,
            own_state_ref[0, h : h + 2],
            got_state_ref[0, h : h + 2].astype(jnp.float32),
        ).reshape(lanes, NSTATE)
        carried = lax.dot_general(
            c_pair[g // 2],
            start.astype(jnp.bfloat16),
            contract_last,
            preferred_element_type=jnp.float32,
        )
        log_pair = jnp.where(first, wide[0], wide[1])
        step_pair = jnp.where(first, step[:, h : h + 1], step[:, h + 1 : h + 2])
        out = jnp.where(first, inner[:seq], inner[seq:]) + jnp.exp(log_pair) * jnp.where(
            first, carried[:seq], carried[seq:]
        )
        out = out + skip_ref[:, span] * values
        z = raw_z_ref[:, span].astype(jnp.float32)
        gated = out * (z / (1.0 + jnp.exp(-z)))
        gated_ref[:, span] = gated
        squares[g // 2] = squares[g // 2] + gated * gated
        last = log_pair[seq - 1 : seq, :]
        scaled = (jnp.exp(last - log_pair) * step_pair * values).astype(jnp.bfloat16)
        added = lax.dot_general(
            scaled, b_pair[g // 2], contract_first, preferred_element_type=jnp.float32
        )
        for i in range(2):
            fade = jnp.exp(wide[i][seq - 1 : seq, :])
            state_ref[0, h + i] = (
                fade * start[i * HDIM : (i + 1) * HDIM]
                + added[i * HDIM : (i + 1) * HDIM, i * NSTATE : (i + 1) * NSTATE]
            )
    total = []
    for value in squares:
        total.append(jnp.sum(jnp.where(first, value, 0.0), axis=1, keepdims=True))
        total.append(jnp.sum(jnp.where(first, 0.0, value), axis=1, keepdims=True))
    part_ref[...] = jnp.concatenate(total, axis=1)


def scan_call(
    slot, mine, lengths, raw_x, raw_z, dt, dt_t, every_bc, own_x, got_x, own_state, got_state,
    conv_x, dt_bias, decay_rate, skip_gain,
):
    requests = lengths.shape[0]
    heads = dt.shape[-1]
    seq = dt.shape[1]
    width = raw_x.shape[1]
    whole = lambda *shape: pl.BlockSpec(shape, lambda q, *_: (0,) * len(shape))
    row = lambda n: pl.BlockSpec((seq, n), lambda q, *_: (q, 0))
    by_q = lambda *shape: pl.BlockSpec((1, *shape), lambda q, *_: (q,) + (0,) * len(shape))
    by_slot = lambda *shape: pl.BlockSpec(
        (1, *shape), lambda q, slots, *_: (slots[q],) + (0,) * len(shape)
    )
    return pl.pallas_call(
        scan_kernel,
        grid_spec=pltpu.PrefetchScalarGridSpec(
            num_scalar_prefetch=3,
            grid=(requests,),
            in_specs=[
                row(width),
                row(width),
                by_q(seq, heads),
                by_q(heads, seq),
                row(every_bc.shape[1]),
                by_slot(KT, width),
                by_q(KT, width),
                by_slot(heads, HDIM, NSTATE),
                by_q(heads, HDIM, NSTATE),
                whole(*conv_x.shape),
                whole(1, heads),
                whole(heads, 1),
                whole(1, heads),
                whole(heads, 1),
                whole(1, width),
            ],
            out_specs=[
                row(width),
                row(GROUPS),
                by_q(heads, HDIM, NSTATE),
                by_q(KT, width),
            ],
            scratch_shapes=[pltpu.VMEM((seq + 16, width), jnp.float32)],
        ),
        out_shape=[
            jax.ShapeDtypeStruct((requests * seq, width), jnp.float32),
            jax.ShapeDtypeStruct((requests * seq, GROUPS), jnp.float32),
            jax.ShapeDtypeStruct((requests, heads, HDIM, NSTATE), jnp.float32),
            jax.ShapeDtypeStruct((requests, KT, width), jnp.bfloat16),
        ],
        compiler_params=pltpu.CompilerParams(vmem_limit_bytes=32 * 1024 * 1024),
        cost_estimate=pl.CostEstimate(
            flops=2 * requests * heads * seq * (seq * HDIM + 2 * HDIM * NSTATE),
            bytes_accessed=requests * heads * HDIM * NSTATE * 10,
            transcendentals=requests * seq * width * 4,
        ),
        name="scan",
    )(
        slot, mine, lengths, raw_x, raw_z, dt, dt_t, every_bc, own_x, got_x, own_state, got_state,
        conv_x, dt_bias[None], dt_bias[:, None], decay_rate[None], decay_rate[:, None],
        jnp.repeat(skip_gain, HDIM)[None],
    )


def local(
    suffix_acts,
    suffix_lens,
    hit_holder,
    hit_slot,
    cache_states,
    cache_conv_x,
    cache_conv_bc,
    w_in_x,
    w_in_z,
    w_in_bc,
    w_in_dt,
    conv_x,
    conv_bc,
    dt_bias,
    decay_rate,
    skip_gain,
    norm_gain,
    w_out,
):
    replica = lax.axis_index("dp")
    lengths = suffix_lens[0]
    requests = lengths.shape[0]
    slot = jnp.where(replica == 0, hit_slot[0], hit_slot[1])
    other_slot = jnp.where(replica == 0, hit_slot[1], hit_slot[0])
    mine = jnp.where(replica == 0, hit_holder[0], hit_holder[1]) == replica
    swap = [(0, 1), (1, 0)]
    got_bc = lax.ppermute(cache_conv_bc[other_slot], "dp", swap)
    got_x = lax.ppermute(cache_conv_x[other_slot], "dp", swap)
    got_state = lax.ppermute(cache_states[other_slot].astype(jnp.bfloat16), "dp", swap)
    tail_bc = jnp.where(mine[:, None, None], cache_conv_bc[slot], got_bc)
    local_x = w_in_x.shape[1]
    local_bc = w_in_bc.shape[1]
    local_heads = w_in_dt.shape[1]
    flat_rows, raw_x, raw_bc, raw_dt = project_call(suffix_acts[0], w_in_x, w_in_bc, w_in_dt)
    seq_len = flat_rows.shape[0] // requests
    raw_bc = raw_bc.reshape(requests, seq_len, local_bc)
    ext_bc, act_bc = causal_conv(tail_bc, raw_bc, conv_bc)
    every_bc = lax.all_gather(
        act_bc.reshape(requests * seq_len, local_bc), "tensor", axis=1, tiled=True
    )
    raw_z = jnp.dot(flat_rows, w_in_z, preferred_element_type=jnp.float32).astype(jnp.bfloat16)
    dt = raw_dt.reshape(requests, seq_len, local_heads)
    new_tail_bc = last_rows(ext_bc, lengths)
    gated, part, new_states, new_tail_x = scan_call(
        slot, mine.astype(jnp.int32), lengths, raw_x, raw_z, dt, dt.transpose(0, 2, 1), every_bc,
        cache_conv_x, got_x, cache_states, got_state, conv_x, dt_bias, decay_rate, skip_gain,
    )
    live = jnp.arange(seq_len, dtype=jnp.int32)[None, :] < lengths[:, None]
    channel = jnp.arange(local_x, dtype=jnp.int32) // HDIM % GROUPS
    member = (jnp.arange(16, dtype=jnp.int32) % 8)[:, None] == channel[None, :]
    mixed_out = output_call(
        gated,
        jnp.pad(part.T, ((0, 8 - GROUPS), (0, 0))),
        live.astype(jnp.float32).reshape(1, -1),
        member.astype(jnp.bfloat16),
        norm_gain[None],
        w_out,
    )
    return (
        mixed_out[None],
        new_states[None],
        new_tail_x[None],
        new_tail_bc[None],
    )


def solution(mesh):
    regular = mesh.shape["tensor"] == 8
    return jax.shard_map(
        local if regular else local_plain,
        mesh=mesh,
        in_specs=(
            P(("groups", "dp"), "tensor", None),
            P(("groups", "dp"), None),
            P("groups", None),
            P("groups", None),
            P(("groups", "dp"), "tensor", None, None),
            P(("groups", "dp"), None, "tensor"),
            P(("groups", "dp"), None, "tensor"),
            P(None, "tensor"),
            P(None, "tensor"),
            P(None, "tensor"),
            P(None, "tensor"),
            P(None, "tensor"),
            P(None, "tensor"),
            P("tensor"),
            P("tensor"),
            P("tensor"),
            P("tensor"),
            P("tensor", None),
        ),
        out_specs=(
            P(("groups", "dp"), "tensor", None),
            P(("groups", "dp"), None, "tensor", None, None),
            P(("groups", "dp"), None, None, "tensor"),
            P(("groups", "dp"), None, None, "tensor"),
        ),
        check_vma=False,
    )
```

```python
import jax
import jax.numpy as jnp
from jax import lax
from jax.experimental import pallas as pl
from jax.experimental.pallas import tpu as pltpu
from jax.sharding import PartitionSpec as P

HEADS = 128
HDIM = 64
NSTATE = 128
GROUPS = 4
KT = 3


highest = lax.Precision.HIGHEST
epsilon = 1e-05


def causal_conv(tail_rows, raw_rows, weight):
    extended = jnp.concatenate([tail_rows, raw_rows], axis=-2)
    seq_len = raw_rows.shape[-2]
    running = jnp.zeros(raw_rows.shape, jnp.float32)
    for offset in range(weight.shape[0]):
        running = running + weight[offset] * extended[..., offset : offset + seq_len, :].astype(
            jnp.float32
        )
    return (extended, lax.optimization_barrier(jax.nn.silu(running).astype(jnp.bfloat16)))


def last_rows(extended, lengths):
    index_rows = lengths[..., None] + jnp.arange(KT, dtype=jnp.int32)
    return jnp.take_along_axis(extended, index_rows[..., None], axis=-2)


def scan_block(values, scores, b_rows, c_rows, step_size, decay_rate, start_state, skip_gain):
    log_step = -decay_rate * step_size
    log_sum = jnp.cumsum(log_step, axis=-2)
    position = jnp.arange(values.shape[-3], dtype=jnp.int32)
    causal = position[:, None] >= position[None, :]
    log_gap = log_sum[..., :, None, :] - log_sum[..., None, :, :]
    decay_mat = jnp.where(causal[:, :, None], jnp.exp(jnp.minimum(log_gap, 0.0)), 0.0)
    weights = scores * decay_mat * step_size[..., None, :, :]
    outputs = jnp.einsum("...tsh,...shp->...thp", weights, values, precision=highest)
    carried = jnp.einsum("...thn,...hpn->...thp", c_rows, start_state, precision=highest)
    outputs = outputs + jnp.exp(log_sum)[..., None] * carried + skip_gain[:, None] * values
    weight_tail = jnp.exp(log_sum[..., -1:, :] - log_sum) * step_size
    scaled_vals = weight_tail[..., None] * values
    end_state = jnp.exp(log_sum[..., -1, :])[..., None, None] * start_state
    end_state = end_state + jnp.einsum(
        "...shp,...shn->...hpn", scaled_vals, b_rows, precision=highest
    )
    return (outputs, end_state)


def local_plain(
    suffix_acts,
    suffix_lens,
    hit_holder,
    hit_slot,
    cache_states,
    cache_conv_x,
    cache_conv_bc,
    w_in_x,
    w_in_z,
    w_in_bc,
    w_in_dt,
    conv_x,
    conv_bc,
    dt_bias,
    decay_rate,
    skip_gain,
    norm_gain,
    w_out,
):
    replica = lax.axis_index("dp")
    lengths = suffix_lens[0]
    requests = lengths.shape[0]
    from_me = hit_holder == replica
    keep_mask = from_me[:, :, None, None]
    send_state = jnp.where(from_me[:, :, None, None, None], cache_states[hit_slot], 0.0)
    send_x = jnp.where(keep_mask, cache_conv_x[hit_slot].astype(jnp.float32), 0.0)
    send_bc = jnp.where(keep_mask, cache_conv_bc[hit_slot].astype(jnp.float32), 0.0)
    got_state, got_x, got_bc = (
        lax.all_to_all(send_state, "dp", split_axis=0, concat_axis=0, tiled=True),
        lax.all_to_all(send_x, "dp", split_axis=0, concat_axis=0, tiled=True),
        lax.all_to_all(send_bc, "dp", split_axis=0, concat_axis=0, tiled=True),
    )
    start_state = jnp.sum(got_state, axis=0)
    tail_x = jnp.sum(got_x, axis=0).astype(jnp.bfloat16)
    tail_bc = jnp.sum(got_bc, axis=0).astype(jnp.bfloat16)
    local_x = w_in_x.shape[1]
    local_bc = w_in_bc.shape[1]
    local_heads = w_in_dt.shape[1]
    flat_rows = lax.all_gather(suffix_acts, "tensor", axis=1, tiled=True)[0]
    pieces = [
        jnp.dot(flat_rows, w_in_x, preferred_element_type=jnp.float32),
        jnp.dot(flat_rows, w_in_z, preferred_element_type=jnp.float32),
        jnp.dot(flat_rows, w_in_bc, preferred_element_type=jnp.float32),
        jnp.dot(flat_rows, w_in_dt, preferred_element_type=jnp.float32),
    ]
    projected = jnp.concatenate(pieces, axis=-1)[None]
    projected = projected[0].reshape(requests, -1, projected.shape[-1])
    seq_len = projected.shape[1]
    raw_x = projected[..., :local_x].astype(jnp.bfloat16)
    raw_z = projected[..., local_x : 2 * local_x].astype(jnp.bfloat16)
    raw_bc = projected[..., 2 * local_x : 2 * local_x + local_bc].astype(jnp.bfloat16)
    raw_x, raw_z, raw_bc = lax.optimization_barrier((raw_x, raw_z, raw_bc))
    raw_dt = projected[..., 2 * local_x + local_bc :]
    ext_x, act_x = causal_conv(tail_x, raw_x, conv_x)
    ext_bc, act_bc = causal_conv(tail_bc, raw_bc, conv_bc)
    new_tail_x = last_rows(ext_x, lengths)
    new_tail_bc = last_rows(ext_bc, lengths)
    every_bc = lax.all_gather(act_bc, "tensor", axis=2, tiled=True)
    half_width = GROUPS * NSTATE
    b_all = every_bc[..., :half_width].reshape(requests, seq_len, GROUPS, NSTATE)
    c_all = every_bc[..., half_width:].reshape(requests, seq_len, GROUPS, NSTATE)
    head_ids = lax.axis_index("tensor") * local_heads + jnp.arange(local_heads, dtype=jnp.int32)
    head_group = head_ids % GROUPS
    group_scores = jnp.einsum("qtgn,qsgn->qtsg", c_all, b_all, preferred_element_type=jnp.float32)
    scores = jnp.take(group_scores, head_group, axis=3)
    b_heads = jnp.take(b_all, head_group, axis=2).astype(jnp.float32)
    c_heads = jnp.take(c_all, head_group, axis=2).astype(jnp.float32)
    live = jnp.arange(seq_len, dtype=jnp.int32)[None, :] < lengths[:, None]
    step_size = jnp.where(live[..., None], jax.nn.softplus(raw_dt + dt_bias), 0.0)
    values = act_x.astype(jnp.float32).reshape(requests, seq_len, local_heads, HDIM)
    outputs, new_states = scan_block(
        values, scores, b_heads, c_heads, step_size, decay_rate, start_state, skip_gain
    )
    gated = outputs * jax.nn.silu(raw_z.astype(jnp.float32)).reshape(
        requests, seq_len, local_heads, HDIM
    )
    per_head = jnp.sum(gated * gated, axis=-1)
    member = (head_group[:, None] == jnp.arange(GROUPS, dtype=jnp.int32)[None, :]).astype(
        jnp.float32
    )
    group_part = jnp.sum(per_head[..., :, None] * member, axis=-2)
    group_total = lax.psum(group_part, "tensor")
    mean_square = jnp.sum(group_total[..., None, :] * member, axis=-1) / (HEADS // GROUPS * HDIM)
    scaled = (
        gated * lax.rsqrt(mean_square + epsilon)[..., None] * norm_gain.reshape(local_heads, HDIM)
    )
    normed = (
        jnp.where(live[..., None, None], scaled, 0.0)
        .astype(jnp.bfloat16)
        .reshape(requests * seq_len, local_x)
    )
    mixed_out = lax.psum_scatter(
        jnp.dot(normed, w_out, preferred_element_type=jnp.float32),
        "tensor",
        scatter_dimension=0,
        tiled=True,
    )
    return (
        mixed_out.astype(jnp.bfloat16)[None],
        new_states[None],
        new_tail_x[None],
        new_tail_bc[None],
    )


LINE = 4


def place():
    me = lax.axis_index("tensor")
    return me, me // 2, me % 2


def nearest(z, k):
    low = z < 2
    near = jnp.where(low, z, LINE - 1 - z)
    pick = jnp.where(near == 0, k, (1, 0, 2, 3)[k])
    return jnp.where(low, pick, LINE - 1 - pick)


def signal(device):
    pl.semaphore_signal(
        pltpu.get_barrier_semaphore(),
        inc=1,
        device_id={"tensor": device},
        device_id_type=pl.DeviceIdType.MESH,
    )


def remote(source, target, send_sem, recv_sem, device):
    return pltpu.make_async_remote_copy(
        src_ref=source,
        dst_ref=target,
        send_sem=send_sem,
        recv_sem=recv_sem,
        device_id={"tensor": device},
        device_id_type=pl.DeviceIdType.MESH,
    )


def project_kernel(
    acts_ref, w_x_ref, w_bc_ref, w_dt_ref, rows_ref, x_ref, bc_ref, dt_ref,
    held, x_buf, bc_buf, dt_buf, load_sem, store_sem, line_send, line_recv, side_send, side_recv,
):
    me, z, y = place()
    part = acts_ref.shape[0]
    side = me + 1 - 2 * y
    loads = [
        pltpu.make_async_copy(acts_ref, held.at[pl.ds(me * part, part)], load_sem.at[0]),
        pltpu.make_async_copy(w_x_ref, x_buf, load_sem.at[1]),
        pltpu.make_async_copy(w_bc_ref, bc_buf, load_sem.at[2]),
        pltpu.make_async_copy(w_dt_ref, dt_buf, load_sem.at[3]),
    ]
    for load in loads:
        load.start()
    signal(side)

    @pl.when(z < LINE - 1)
    def _():
        signal(me + 2)

    @pl.when(z > 0)
    def _():
        signal(me - 2)

    ends = (z == 0) | (z == LINE - 1)
    pl.semaphore_wait(pltpu.get_barrier_semaphore(), jnp.where(ends, 2, 3))

    def spot(plane, column):
        return held.at[pl.ds((2 * plane + column) * part, part)]

    def up(plane):
        return remote(
            spot(plane, y), spot(plane, y), line_send.at[0, plane], line_recv.at[plane], me + 2
        )

    def down(plane):
        return remote(
            spot(plane, y), spot(plane, y), line_send.at[1, plane], line_recv.at[plane], me - 2
        )

    def across(plane):
        return remote(
            spot(plane, y), spot(plane, y), side_send.at[plane], side_recv.at[plane], side
        )

    def arrived(plane, column, sem):
        return remote(spot(plane, column), spot(plane, column), line_send.at[0, 0], sem, side)

    loads[0].wait()
    for k in range(LINE + 1):
        if k < LINE:
            plane = nearest(z, k)
            if k > 0:
                arrived(plane, y, line_recv.at[plane]).wait_recv()

            @pl.when((plane <= z) & (z < LINE - 1))
            def _():
                up(plane).start()

            @pl.when((plane >= z) & (z > 0))
            def _():
                down(plane).start()

            across(plane).start()
        if k == 1:
            for load in loads[1:]:
                load.wait()
        if k > 0:
            plane = nearest(z, k - 1)
            arrived(plane, 1 - y, side_recv.at[plane]).wait_recv()
            span = pl.ds(plane * (2 * part), 2 * part)
            pltpu.make_async_copy(held.at[span], rows_ref.at[span], store_sem.at[k - 1]).start()
            bc_ref[span, :] = jnp.dot(
                held[span, :], bc_buf[...], preferred_element_type=jnp.float32
            ).astype(jnp.bfloat16)
            dt_ref[span, :] = jnp.dot(
                held[span, :], dt_buf[...], preferred_element_type=jnp.float32
            )
            tile = 256

            def step(j, carry):
                columns = pl.ds(pl.multiple_of(j * tile, tile), tile)
                x_ref[span, columns] = jnp.dot(
                    held[span, :], x_buf[:, columns], preferred_element_type=jnp.float32
                ).astype(jnp.bfloat16)
                return carry

            lax.fori_loop(0, x_ref.shape[1] // tile, step, 0)
    for k in range(LINE):
        plane = nearest(z, k)

        @pl.when((plane <= z) & (z < LINE - 1))
        def _():
            up(plane).wait_send()

        @pl.when((plane >= z) & (z > 0))
        def _():
            down(plane).wait_send()

        across(plane).wait_send()
        span = pl.ds(plane * (2 * part), 2 * part)
        pltpu.make_async_copy(held.at[span], rows_ref.at[span], store_sem.at[k]).wait()


def project_call(acts, w_x, w_bc, w_dt):
    part, depth = acts.shape
    rows = part * 2 * LINE
    vmem = pl.BlockSpec(memory_space=pltpu.VMEM)
    hbm = pl.BlockSpec(memory_space=pl.ANY)
    dma = pltpu.SemaphoreType.DMA
    return pl.pallas_call(
        project_kernel,
        in_specs=[hbm] * 4,
        out_specs=[hbm, vmem, vmem, vmem],
        out_shape=[
            jax.ShapeDtypeStruct((rows, depth), jnp.bfloat16),
            jax.ShapeDtypeStruct((rows, w_x.shape[1]), jnp.bfloat16),
            jax.ShapeDtypeStruct((rows, w_bc.shape[1]), jnp.bfloat16),
            jax.ShapeDtypeStruct((rows, w_dt.shape[1]), jnp.float32),
        ],
        scratch_shapes=[
            pltpu.VMEM((rows, depth), jnp.bfloat16),
            pltpu.VMEM(w_x.shape, jnp.bfloat16),
            pltpu.VMEM(w_bc.shape, jnp.bfloat16),
            pltpu.VMEM(w_dt.shape, jnp.bfloat16),
            dma((4,)),
            dma((LINE,)),
            dma((2, LINE)),
            dma((LINE,)),
            dma((LINE,)),
            dma((LINE,)),
        ],
        compiler_params=pltpu.CompilerParams(
            collective_id=0, has_side_effects=True, vmem_limit_bytes=40 * 1024 * 1024
        ),
        cost_estimate=pl.CostEstimate(
            flops=2 * rows * depth * w_x.shape[1],
            bytes_accessed=4 * rows * depth + 2 * depth * w_x.shape[1],
            transcendentals=0,
        ),
        name="gather_project",
    )(acts, w_x, w_bc, w_dt)


def gate_kernel(
    bc_ref, rows_ref, w_ref, every_ref, z_ref,
    held, rows_buf, w_buf, load_sem, store_sem, line_send, line_recv, side_send, side_recv,
):
    me, z, y = place()
    side = me + 1 - 2 * y
    loads = [
        pltpu.make_async_copy(bc_ref, held.at[me], load_sem.at[0]),
        pltpu.make_async_copy(w_ref, w_buf, load_sem.at[1]),
        pltpu.make_async_copy(rows_ref, rows_buf, load_sem.at[2]),
    ]
    for load in loads:
        load.start()
    signal(side)

    @pl.when(z < LINE - 1)
    def _():
        signal(me + 2)

    @pl.when(z > 0)
    def _():
        signal(me - 2)

    ends = (z == 0) | (z == LINE - 1)
    pl.semaphore_wait(pltpu.get_barrier_semaphore(), jnp.where(ends, 2, 3))

    def spot(plane, column):
        return held.at[2 * plane + column]

    def up(plane):
        return remote(
            spot(plane, y), spot(plane, y), line_send.at[0, plane], line_recv.at[plane], me + 2
        )

    def down(plane):
        return remote(
            spot(plane, y), spot(plane, y), line_send.at[1, plane], line_recv.at[plane], me - 2
        )

    def across(plane):
        return remote(
            spot(plane, y), spot(plane, y), side_send.at[plane], side_recv.at[plane], side
        )

    def arrived(plane, column, sem):
        return remote(spot(plane, column), spot(plane, column), line_send.at[0, 0], sem, side)

    loads[0].wait()
    for k in range(LINE + 1):
        if k < LINE:
            plane = nearest(z, k)
            if k > 0:
                arrived(plane, y, line_recv.at[plane]).wait_recv()

            @pl.when((plane <= z) & (z < LINE - 1))
            def _():
                up(plane).start()

            @pl.when((plane >= z) & (z > 0))
            def _():
                down(plane).start()

            across(plane).start()
        if k == 1:
            for load in loads[1:]:
                load.wait()
        if k > 0:
            share = rows_buf.shape[0] // LINE
            span = slice((k - 1) * share, k * share)
            tile = 256

            def step(j, carry):
                columns = pl.ds(pl.multiple_of(j * tile, tile), tile)
                z_ref[span, columns] = jnp.dot(
                    rows_buf[span, :], w_buf[:, columns], preferred_element_type=jnp.float32
                ).astype(jnp.bfloat16)
                return carry

            lax.fori_loop(0, z_ref.shape[1] // tile, step, 0)
    for k in range(LINE):
        plane = nearest(z, k)

        @pl.when((plane <= z) & (z < LINE - 1))
        def _():
            up(plane).wait_send()

        @pl.when((plane >= z) & (z > 0))
        def _():
            down(plane).wait_send()

        across(plane).wait_send()
        arrived(plane, 1 - y, side_recv.at[plane]).wait_recv()
    store = pltpu.make_async_copy(held, every_ref, store_sem)
    store.start()
    store.wait()


def gate_call(bc, flat_rows, w_z):
    rows, depth = flat_rows.shape
    hbm = pl.BlockSpec(memory_space=pl.ANY)
    dma = pltpu.SemaphoreType.DMA
    return pl.pallas_call(
        gate_kernel,
        in_specs=[hbm] * 3,
        out_specs=[hbm, pl.BlockSpec(memory_space=pltpu.VMEM)],
        out_shape=[
            jax.ShapeDtypeStruct((2 * LINE, *bc.shape), jnp.bfloat16),
            jax.ShapeDtypeStruct((rows, w_z.shape[1]), jnp.bfloat16),
        ],
        scratch_shapes=[
            pltpu.VMEM((2 * LINE, *bc.shape), jnp.bfloat16),
            pltpu.VMEM(flat_rows.shape, jnp.bfloat16),
            pltpu.VMEM(w_z.shape, jnp.bfloat16),
            dma((3,)),
            dma,
            dma((2, LINE)),
            dma((LINE,)),
            dma((LINE,)),
            dma((LINE,)),
        ],
        compiler_params=pltpu.CompilerParams(
            collective_id=2, has_side_effects=True, vmem_limit_bytes=40 * 1024 * 1024
        ),
        name="gather_gate",
    )(bc, flat_rows, w_z)


def output_kernel(
    gated_ref, part_ref, live_ref, member_ref, gain_ref, w_ref, out_ref,
    parts, normed, w_buf, own, side_out, side_in, line_out, line_in,
    load_sem, part_send, part_recv, side_send, side_recv, line_send, line_recv,
):
    me, z, y = place()
    peers = 2 * LINE
    rows, width = gated_ref.shape
    chunk = rows // peers
    side = me + 1 - 2 * y
    load = pltpu.make_async_copy(w_ref, w_buf, load_sem)
    load.start()
    for hop in range(1, peers):
        signal(lax.rem(me + hop, peers))
    pl.semaphore_wait(pltpu.get_barrier_semaphore(), peers - 1)
    sends = []
    for hop in range(1, peers):
        send = remote(
            part_ref, parts.at[hop], part_send.at[hop], part_recv.at[hop], lax.rem(me + hop, peers)
        )
        send.start()
        sends.append(send)
    total = part_ref[...]
    for hop in range(1, peers):
        sends[hop - 1].wait_recv()
        total = total + parts[hop]
    inverse = lax.rsqrt(total / (HEADS // GROUPS * HDIM) + epsilon)
    inverse = jnp.where(live_ref[...] > 0.0, inverse, 0.0)
    high = inverse.astype(jnp.bfloat16)
    low = (inverse - high.astype(jnp.float32)).astype(jnp.bfloat16)
    both = jnp.concatenate([high, low], axis=0)
    block = rows // 2
    for i in range(2):
        scale = lax.dot_general(
            both[:, i * block : (i + 1) * block],
            member_ref[...],
            (((0,), (0,)), ((), ())),
            preferred_element_type=jnp.float32,
        )
        span = slice(i * block, (i + 1) * block)
        normed[span, :] = (gated_ref[span, :] * scale * gain_ref[...]).astype(jnp.bfloat16)
    load.wait()

    def across(plane):
        return remote(
            side_out.at[plane], side_in.at[plane], side_send.at[plane], side_recv.at[plane], side
        )

    def along(plane):
        toward = jnp.where(plane > z, me + 2, me - 2)
        slot = jnp.where((plane < z) & (plane == z - 1), LINE, plane)
        return remote(
            line_out.at[plane], line_in.at[slot], line_send.at[plane], line_recv.at[slot], toward
        )

    def line_arrived(slot):
        return remote(line_in.at[slot], line_in.at[slot], line_send.at[0], line_recv.at[slot], side)

    tile = 512
    tiles = w_buf.shape[1] // tile
    for k in range(LINE - 1, -1, -1):
        plane = nearest(z, k)
        span = pl.ds(plane * (2 * chunk), 2 * chunk)

        def step(j, carry):
            columns = pl.ds(pl.multiple_of(j * tile, tile), tile)
            result = jnp.dot(
                normed[span, :], w_buf[:, columns], preferred_element_type=jnp.float32
            )
            own[plane, :, columns] = jnp.where(y == 0, result[:chunk], result[chunk:])
            side_out[plane, :, columns] = jnp.where(
                y == 0, result[chunk:], result[:chunk]
            ).astype(jnp.bfloat16)
            return carry

        lax.fori_loop(0, tiles, step, 0)
        across(plane).start()
    for k in range(LINE - 1, 0, -1):
        plane = nearest(z, k)
        across(plane).wait_recv()
        joined = ((plane > z) & (z > 0)) | ((plane < z) & (z < LINE - 1))

        @pl.when(joined)
        def _():
            line_arrived(plane).wait_recv()
            line_out[plane] = (
                own[plane]
                + side_in[plane].astype(jnp.float32)
                + line_in[plane].astype(jnp.float32)
            ).astype(jnp.bfloat16)

        @pl.when(jnp.logical_not(joined))
        def _():
            line_out[plane] = (own[plane] + side_in[plane].astype(jnp.float32)).astype(
                jnp.bfloat16
            )

        along(plane).start()
    across(z).wait_recv()
    own[z] = own[z] + side_in[z].astype(jnp.float32)

    @pl.when(z > 0)
    def _():
        line_arrived(z).wait_recv()
        own[z] = own[z] + line_in[z].astype(jnp.float32)

    @pl.when(z < LINE - 1)
    def _():
        line_arrived(LINE).wait_recv()
        own[z] = own[z] + line_in[LINE].astype(jnp.float32)

    out_ref[...] = own[z].astype(jnp.bfloat16)
    for send in sends:
        send.wait_send()
    for k in range(LINE):
        plane = nearest(z, k)
        across(plane).wait_send()
        if k > 0:
            along(plane).wait_send()


def output_call(gated, part, live, member, gain, w_out):
    rows, width = gated.shape
    depth = w_out.shape[1]
    peers = 2 * LINE
    chunk = rows // peers
    vmem = pl.BlockSpec(memory_space=pltpu.VMEM)
    dma = pltpu.SemaphoreType.DMA
    return pl.pallas_call(
        output_kernel,
        in_specs=[vmem] * 5 + [pl.BlockSpec(memory_space=pl.ANY)],
        out_specs=vmem,
        out_shape=jax.ShapeDtypeStruct((chunk, depth), jnp.bfloat16),
        scratch_shapes=[
            pltpu.VMEM((peers, *part.shape), jnp.float32),
            pltpu.VMEM((rows, width), jnp.bfloat16),
            pltpu.VMEM(w_out.shape, jnp.bfloat16),
            pltpu.VMEM((LINE, chunk, depth), jnp.float32),
            pltpu.VMEM((LINE, chunk, depth), jnp.bfloat16),
            pltpu.VMEM((LINE, chunk, depth), jnp.bfloat16),
            pltpu.VMEM((LINE, chunk, depth), jnp.bfloat16),
            pltpu.VMEM((LINE + 1, chunk, depth), jnp.bfloat16),
            dma,
            dma((peers,)),
            dma((peers,)),
            dma((LINE,)),
            dma((LINE,)),
            dma((LINE,)),
            dma((LINE + 1,)),
        ],
        compiler_params=pltpu.CompilerParams(
            collective_id=1, has_side_effects=True, vmem_limit_bytes=52 * 1024 * 1024
        ),
        cost_estimate=pl.CostEstimate(
            flops=2 * rows * width * depth,
            bytes_accessed=2 * width * depth + 4 * rows * width,
            transcendentals=0,
        ),
        name="norm_project_reduce",
    )(gated, part, live, member, gain, w_out)


def scan_kernel(
    slot_ref,
    mine_ref,
    len_ref,
    raw_x_ref,
    raw_z_ref,
    dt_ref,
    dt_t_ref,
    bc_ref,
    own_x_ref,
    got_x_ref,
    own_state_ref,
    got_state_ref,
    conv_ref,
    bias_ref,
    bias_t_ref,
    decay_ref,
    decay_t_ref,
    skip_ref,
    gated_ref,
    part_ref,
    state_ref,
    tail_ref,
    ext_ref,
):
    q = pl.program_id(0)
    mine = mine_ref[q] == 1
    length = len_ref[q]
    seq, width = raw_x_ref.shape
    heads = dt_ref.shape[-1]
    pad = 8
    tail = jnp.where(
        mine, own_x_ref[0].astype(jnp.float32), got_x_ref[0].astype(jnp.float32)
    )
    ext_ref[0:pad, :] = jnp.zeros((pad, width), jnp.float32)
    ext_ref[pl.ds(pad - KT, KT), :] = tail
    ext_ref[pl.ds(pad, seq), :] = raw_x_ref[...].astype(jnp.float32)
    picked = lax.broadcasted_iota(jnp.int32, (pad, pad + seq), 1) == (
        lax.broadcasted_iota(jnp.int32, (pad, pad + seq), 0) + (pad - KT + length)
    )
    tail_ref[0] = jnp.dot(
        picked.astype(jnp.bfloat16),
        ext_ref[0 : pad + seq, :].astype(jnp.bfloat16),
        preferred_element_type=jnp.float32,
    )[:KT].astype(jnp.bfloat16)

    step = jnp.where(
        lax.broadcasted_iota(jnp.int32, (seq, heads), 0) < length,
        jax.nn.softplus(dt_ref[0] + bias_ref[...]),
        0.0,
    )
    step_t = jnp.where(
        lax.broadcasted_iota(jnp.int32, (heads, seq), 1) < length,
        jax.nn.softplus(dt_t_ref[0] + bias_t_ref[...]),
        0.0,
    )
    rows = lax.broadcasted_iota(jnp.int32, (seq, seq), 0)
    cols = lax.broadcasted_iota(jnp.int32, (seq, seq), 1)
    causal = rows >= cols
    log_sum = jnp.dot(
        causal.astype(jnp.float32),
        -decay_ref[...] * step,
        precision=highest,
        preferred_element_type=jnp.float32,
    )
    log_sum_t = jnp.dot(
        -decay_t_ref[...] * step_t,
        (rows <= cols).astype(jnp.float32),
        precision=highest,
        preferred_element_type=jnp.float32,
    )
    contract_last = (((1,), (1,)), ((), ()))
    contract_first = (((0,), (0,)), ((), ()))
    b_rows = [bc_ref[g] for g in range(GROUPS)]
    c_rows = [bc_ref[GROUPS + g] for g in range(GROUPS)]
    scores = [
        lax.dot_general(
            c_rows[g], b_rows[g], contract_last, preferred_element_type=jnp.float32
        )
        for g in range(GROUPS)
    ]
    c_pair = [jnp.concatenate([c_rows[g], c_rows[g + 1]], axis=0) for g in range(0, GROUPS, 2)]
    b_pair = [jnp.concatenate([b_rows[g], b_rows[g + 1]], axis=1) for g in range(0, GROUPS, 2)]
    lanes = 2 * HDIM
    first = lax.broadcasted_iota(jnp.int32, (seq, lanes), 1) < HDIM
    squares = [jnp.zeros((seq, lanes), jnp.float32) for _ in range(GROUPS // 2)]
    for pair in range(heads // 2):
        h = 2 * pair
        g = h % GROUPS
        span = slice(pair * lanes, (pair + 1) * lanes)
        running = conv_ref[0:1, span] * ext_ref[pad - KT : pad - KT + seq, span]
        for k in range(1, KT + 1):
            running = running + (
                conv_ref[k : k + 1, span] * ext_ref[pad - KT + k : pad - KT + k + seq, span]
            )
        act = (running / (1.0 + jnp.exp(-running))).astype(jnp.bfloat16)
        values = act.astype(jnp.float32)
        wide = [jnp.broadcast_to(log_sum[:, h + i : h + i + 1], (seq, lanes)) for i in range(2)]
        mats = []
        for i in range(2):
            gap = jnp.minimum(wide[i][:, :seq] - log_sum_t[h + i : h + i + 1, :], 0.0)
            decay = jnp.where(causal, jnp.exp(gap), 0.0)
            mats.append(
                (scores[g + i] * decay * step_t[h + i : h + i + 1, :]).astype(jnp.bfloat16)
            )
        inner = jnp.dot(
            jnp.concatenate(mats, axis=0), act, preferred_element_type=jnp.float32
        )
        start = jnp.where(
            mine,
            own_state_ref[0, h : h + 2],
            got_state_ref[0, h : h + 2].astype(jnp.float32),
        ).reshape(lanes, NSTATE)
        carried = lax.dot_general(
            c_pair[g // 2],
            start.astype(jnp.bfloat16),
            contract_last,
            preferred_element_type=jnp.float32,
        )
        log_pair = jnp.where(first, wide[0], wide[1])
        step_pair = jnp.where(first, step[:, h : h + 1], step[:, h + 1 : h + 2])
        out = jnp.where(first, inner[:seq], inner[seq:]) + jnp.exp(log_pair) * jnp.where(
            first, carried[:seq], carried[seq:]
        )
        out = out + skip_ref[:, span] * values
        z = raw_z_ref[:, span].astype(jnp.float32)
        gated = out * (z / (1.0 + jnp.exp(-z)))
        gated_ref[:, span] = gated
        squares[g // 2] = squares[g // 2] + gated * gated
        last = log_pair[seq - 1 : seq, :]
        scaled = (jnp.exp(last - log_pair) * step_pair * values).astype(jnp.bfloat16)
        added = lax.dot_general(
            scaled, b_pair[g // 2], contract_first, preferred_element_type=jnp.float32
        )
        for i in range(2):
            fade = jnp.exp(wide[i][seq - 1 : seq, :])
            state_ref[0, h + i] = (
                fade * start[i * HDIM : (i + 1) * HDIM]
                + added[i * HDIM : (i + 1) * HDIM, i * NSTATE : (i + 1) * NSTATE]
            )
    total = []
    for value in squares:
        total.append(jnp.sum(jnp.where(first, value, 0.0), axis=1, keepdims=True))
        total.append(jnp.sum(jnp.where(first, 0.0, value), axis=1, keepdims=True))
    part_ref[...] = jnp.concatenate(total, axis=1)


def scan_call(
    slot, mine, lengths, raw_x, raw_z, dt, dt_t, every_bc, own_x, got_x, own_state, got_state,
    conv_x, dt_bias, decay_rate, skip_gain,
):
    requests = lengths.shape[0]
    heads = dt.shape[-1]
    seq = dt.shape[1]
    width = raw_x.shape[1]
    whole = lambda *shape: pl.BlockSpec(shape, lambda q, *_: (0,) * len(shape))
    row = lambda n: pl.BlockSpec((seq, n), lambda q, *_: (q, 0))
    by_q = lambda *shape: pl.BlockSpec((1, *shape), lambda q, *_: (q,) + (0,) * len(shape))
    by_slot = lambda *shape: pl.BlockSpec(
        (1, *shape), lambda q, slots, *_: (slots[q],) + (0,) * len(shape)
    )
    return pl.pallas_call(
        scan_kernel,
        grid_spec=pltpu.PrefetchScalarGridSpec(
            num_scalar_prefetch=3,
            grid=(requests,),
            in_specs=[
                row(width),
                row(width),
                by_q(seq, heads),
                by_q(heads, seq),
                pl.BlockSpec((every_bc.shape[0], seq, NSTATE), lambda q, *_: (0, q, 0)),
                by_slot(KT, width),
                by_q(KT, width),
                by_slot(heads, HDIM, NSTATE),
                by_q(heads, HDIM, NSTATE),
                whole(*conv_x.shape),
                whole(1, heads),
                whole(heads, 1),
                whole(1, heads),
                whole(heads, 1),
                whole(1, width),
            ],
            out_specs=[
                row(width),
                row(GROUPS),
                by_q(heads, HDIM, NSTATE),
                by_q(KT, width),
            ],
            scratch_shapes=[pltpu.VMEM((seq + 16, width), jnp.float32)],
        ),
        out_shape=[
            jax.ShapeDtypeStruct((requests * seq, width), jnp.float32),
            jax.ShapeDtypeStruct((requests * seq, GROUPS), jnp.float32),
            jax.ShapeDtypeStruct((requests, heads, HDIM, NSTATE), jnp.float32),
            jax.ShapeDtypeStruct((requests, KT, width), jnp.bfloat16),
        ],
        compiler_params=pltpu.CompilerParams(vmem_limit_bytes=32 * 1024 * 1024),
        cost_estimate=pl.CostEstimate(
            flops=2 * requests * heads * seq * (seq * HDIM + 2 * HDIM * NSTATE),
            bytes_accessed=requests * heads * HDIM * NSTATE * 10,
            transcendentals=requests * seq * width * 4,
        ),
        name="scan",
    )(
        slot, mine, lengths, raw_x, raw_z, dt, dt_t, every_bc, own_x, got_x, own_state, got_state,
        conv_x, dt_bias[None], dt_bias[:, None], decay_rate[None], decay_rate[:, None],
        jnp.repeat(skip_gain, HDIM)[None],
    )


def local(
    suffix_acts,
    suffix_lens,
    hit_holder,
    hit_slot,
    cache_states,
    cache_conv_x,
    cache_conv_bc,
    w_in_x,
    w_in_z,
    w_in_bc,
    w_in_dt,
    conv_x,
    conv_bc,
    dt_bias,
    decay_rate,
    skip_gain,
    norm_gain,
    w_out,
):
    replica = lax.axis_index("dp")
    lengths = suffix_lens[0]
    requests = lengths.shape[0]
    slot = jnp.where(replica == 0, hit_slot[0], hit_slot[1])
    other_slot = jnp.where(replica == 0, hit_slot[1], hit_slot[0])
    mine = jnp.where(replica == 0, hit_holder[0], hit_holder[1]) == replica
    swap = [(0, 1), (1, 0)]
    got_bc = lax.ppermute(cache_conv_bc[other_slot], "dp", swap)
    got_x = lax.ppermute(cache_conv_x[other_slot], "dp", swap)
    got_state = lax.ppermute(cache_states[other_slot].astype(jnp.bfloat16), "dp", swap)
    tail_bc = jnp.where(mine[:, None, None], cache_conv_bc[slot], got_bc)
    local_x = w_in_x.shape[1]
    local_bc = w_in_bc.shape[1]
    local_heads = w_in_dt.shape[1]
    flat_rows, raw_x, raw_bc, raw_dt = project_call(suffix_acts[0], w_in_x, w_in_bc, w_in_dt)
    seq_len = flat_rows.shape[0] // requests
    raw_bc = raw_bc.reshape(requests, seq_len, local_bc)
    ext_bc, act_bc = causal_conv(tail_bc, raw_bc, conv_bc)
    every_bc, raw_z = gate_call(
        act_bc.reshape(requests * seq_len, local_bc), flat_rows, w_in_z
    )
    dt = raw_dt.reshape(requests, seq_len, local_heads)
    new_tail_bc = last_rows(ext_bc, lengths)
    gated, part, new_states, new_tail_x = scan_call(
        slot, mine.astype(jnp.int32), lengths, raw_x, raw_z, dt, dt.transpose(0, 2, 1), every_bc,
        cache_conv_x, got_x, cache_states, got_state, conv_x, dt_bias, decay_rate, skip_gain,
    )
    live = jnp.arange(seq_len, dtype=jnp.int32)[None, :] < lengths[:, None]
    channel = jnp.arange(local_x, dtype=jnp.int32) // HDIM % GROUPS
    member = (jnp.arange(16, dtype=jnp.int32) % 8)[:, None] == channel[None, :]
    mixed_out = output_call(
        gated,
        jnp.pad(part.T, ((0, 8 - GROUPS), (0, 0))),
        live.astype(jnp.float32).reshape(1, -1),
        member.astype(jnp.bfloat16),
        norm_gain[None],
        w_out,
    )
    return (
        mixed_out[None],
        new_states[None],
        new_tail_x[None],
        new_tail_bc[None],
    )


def solution(mesh):
    regular = mesh.shape["tensor"] == 8
    return jax.shard_map(
        local if regular else local_plain,
        mesh=mesh,
        in_specs=(
            P(("groups", "dp"), "tensor", None),
            P(("groups", "dp"), None),
            P("groups", None),
            P("groups", None),
            P(("groups", "dp"), "tensor", None, None),
            P(("groups", "dp"), None, "tensor"),
            P(("groups", "dp"), None, "tensor"),
            P(None, "tensor"),
            P(None, "tensor"),
            P(None, "tensor"),
            P(None, "tensor"),
            P(None, "tensor"),
            P(None, "tensor"),
            P("tensor"),
            P("tensor"),
            P("tensor"),
            P("tensor"),
            P("tensor", None),
        ),
        out_specs=(
            P(("groups", "dp"), "tensor", None),
            P(("groups", "dp"), None, "tensor", None, None),
            P(("groups", "dp"), None, None, "tensor"),
            P(("groups", "dp"), None, None, "tensor"),
        ),
        check_vma=False,
    )
```
